256 devices in a mesh: px: 16 (over y, x), py: 8 (over z), pair: 2 (over core).
Axes of the slice: x: 4, y: 4, z: 8, core: 2. Of those that a mesh axis runs over, the one named last changes fastest.
Arguments:
- fields: bfloat16 [2, 64, 64, 64, 128], P('pair', None, 'px', 'py'), may hold values from -6 to 6
- cotangent: bfloat16 [2, 64, 64, 64, 128], P('pair', None, 'px', 'py'), may hold values from -6 to 6
- spectral_weight: bfloat16 [16, 16, 16, 64, 128], P('px', 'py'), may hold values from -0.5 to 0.5
- local_weight: bfloat16 [64, 64], replicated, may hold values from -0.75 to 0.75
- bias_term: float32 [64], replicated, may hold values from -1 to 1
Outputs:
- activation: bfloat16 [2, 64, 64, 64, 128], P('pair', None, 'px', 'py')
- input_grad: bfloat16 [2, 64, 64, 64, 128], P('pair', None, 'px', 'py')
- weight_grad: float32 [16, 16, 16, 64, 128], P('px', 'py')
The draws below stay inside these ranges and needn't reach their ends.
All inputs are finite; a program needn't handle non-finite values.
Results may differ from the reference program's by a relative error of at most 0.0053.
Values sent between devices are 32-bit elements; how exact they have to be, the bound alone decides.
No kernel may reach another device: no remote copies, remote signals or barrier semaphores. Data moves between devices by JAX's collectives and lax.ppermute only.
A program may use at most 64 MiB of HBM per device.

```python
import math
import jax
import jax.numpy as jnp
from jax import lax

C = 64
KX = 16
KY = 16
KZ = 16
NZ = 128
NX = 64
NY = 64
SAMPLES = 2
N_PAIR = 2


def block_scale(own_key, shape, pieces, smallest, top_value):
    def one(position, blocks):
        draws = jax.random.uniform(jax.random.fold_in(jax.random.fold_in(own_key, 6), position), (blocks,), jnp.float32, smallest / len(pieces), top_value / len(pieces))
        return jnp.repeat(jnp.exp(draws), shape[position] // blocks).reshape((-1,) + (1,) * (len(shape) - position - 1))

    gain = one(*pieces[0])
    for cut in pieces[1:]:
        gain = gain * one(*cut)
    return gain


def bell_draw(rng, extent, deviation, bound, split=(), kind=jnp.bfloat16):
    array = deviation * jax.random.normal(rng, extent, jnp.float32)
    if split:
        array = array * block_scale(rng, extent, split, -0.22, 0.18)
    return jnp.clip(array, -bound, bound).astype(kind)


def setup_inputs(seed: int = 0) -> dict:
    splits = jax.random.split(jax.random.key(seed), 6)
    fields = bell_draw(splits[0], (SAMPLES, C, NX, NY, NZ), 1.0, 6.0, ((0, 2), (2, 16), (3, 8)))
    cotangent = bell_draw(splits[1], (SAMPLES, C, NX, NY, NZ), 1.0, 6.0, ((0, 2), (2, 16), (3, 8)))
    spectral_weight = bell_draw(splits[2], (KY, KZ, KX, C, 2 * C), (2 * C) ** -0.5, 0.5, ((0, 16), (1, 8)))
    local_weight = bell_draw(splits[3], (C, C), C ** -0.5, 0.75)
    bias_term = jnp.clip(jax.random.uniform(splits[4], (C,), jnp.float32, -1.0, 1.0), -1.0, 1.0)
    return {"fields": fields, "cotangent": cotangent, "spectral_weight": spectral_weight, "local_weight": local_weight, "bias_term": bias_term}


HIGHEST = lax.Precision.HIGHEST

def angle_table(modes_count, first_cell, cell_count, length):
    cells = first_cell + jnp.arange(cell_count, dtype=jnp.int32)
    waves = jnp.arange(modes_count, dtype=jnp.int32)
    phases = cells[:, None] * waves[None, :] % length
    return phases.astype(jnp.float32) * (2.0 * math.pi / length)

def turn_modes(values, cosine_table, sine_table, formula):
    half_width = values.shape[-1] // 2
    real_part = values[..., :half_width]
    imag_part = values[..., half_width:]

    def contract(operand, table):
        return jnp.einsum(formula, operand, table, precision=HIGHEST)
    first = contract(real_part, cosine_table) + contract(imag_part, sine_table)
    second = contract(imag_part, cosine_table) - contract(real_part, sine_table)
    return jnp.concatenate([first, second], axis=-1)

def depth_section(field_in):
    chans, width_x, width_y, depth = field_in.shape
    angles = angle_table(KZ, 0, depth, depth)
    table = jnp.stack([jnp.cos(angles), -jnp.sin(angles)], axis=1).astype(jnp.bfloat16)
    flat = jnp.dot(field_in.reshape(chans * width_x * width_y, depth), table.reshape(depth, 2 * KZ), preferred_element_type=jnp.float32)
    sectioned = jnp.transpose(flat.reshape(chans, width_x, width_y, 2, KZ), (1, 2, 4, 3, 0))
    return sectioned.reshape(width_x, width_y, KZ, 2 * chans)

def channel_mix(matrix, field_in):
    chans = field_in.shape[0]
    flat = jnp.dot(matrix, field_in.reshape(chans, -1), preferred_element_type=jnp.float32)
    return flat.reshape(field_in.shape)

def depth_back(values, formula):
    half_width = values.shape[-1] // 2
    angles = angle_table(KZ, 0, NZ, NZ)
    real_out = jnp.einsum(formula, values[..., :half_width], jnp.cos(angles), precision=HIGHEST)
    imag_out = jnp.einsum(formula, values[..., half_width:], jnp.sin(angles), precision=HIGHEST)
    return real_out - imag_out

def forward_transform(field_in, factor):
    sectioned = depth_section(field_in)
    y_angles = angle_table(KY, 0, NY, NY)
    sectioned = turn_modes(sectioned, jnp.cos(y_angles), jnp.sin(y_angles), 'xyzc,yk->xkzc')
    x_angles = angle_table(KX, 0, NX, NX)
    sectioned = turn_modes(sectioned, jnp.cos(x_angles), jnp.sin(x_angles), 'xyzc,xj->yzjc')
    return sectioned * factor

def inverse_transform(spectrum, factor):
    x_angles = angle_table(KX, 0, NX, NX)
    wide = turn_modes(spectrum, jnp.cos(x_angles), -jnp.sin(x_angles), 'yzjc,xj->xyzc')
    y_angles = angle_table(KY, 0, NY, NY)

    def one_plane(plane):
        column = turn_modes(plane, jnp.cos(y_angles), -jnp.sin(y_angles), 'kzc,yk->yzc')
        return depth_back(column, 'ykc,zk->cyz')
    planes = lax.map(one_plane, wide)
    return jnp.transpose(planes, (1, 0, 2, 3)) * factor

def mix_modes(spectrum, weight):
    half_width = spectrum.shape[-1] // 2
    weight_full = weight.astype(jnp.float32)
    rotated = jnp.concatenate([-weight_full[..., half_width:], weight_full[..., :half_width]], axis=-1)
    first = jnp.einsum('...c,...cd->...d', spectrum[..., :half_width], weight_full, precision=HIGHEST)
    return first + jnp.einsum('...c,...cd->...d', spectrum[..., half_width:], rotated, precision=HIGHEST)

def mix_back(grad_spec, weight):
    half_width = grad_spec.shape[-1] // 2
    weight_full = weight.astype(jnp.float32)
    turned = jnp.concatenate([grad_spec[..., half_width:], -grad_spec[..., :half_width]], axis=-1)
    real_out = jnp.einsum('...d,...cd->...c', grad_spec, weight_full, precision=HIGHEST)
    imag_out = jnp.einsum('...d,...cd->...c', turned, weight_full, precision=HIGHEST)
    return jnp.concatenate([real_out, imag_out], axis=-1)

def weight_term(spectrum, grad_spec):
    half_width = spectrum.shape[-1] // 2
    turned = jnp.concatenate([grad_spec[..., half_width:], -grad_spec[..., :half_width]], axis=-1)
    first = jnp.einsum('...c,...d->...cd', spectrum[..., :half_width], grad_spec, precision=HIGHEST)
    return first + jnp.einsum('...c,...d->...cd', spectrum[..., half_width:], turned, precision=HIGHEST)

def gelu_slope(pre):
    cumulative = 0.5 * (1.0 + lax.erf(pre / math.sqrt(2.0)))
    density = jnp.exp(-0.5 * pre * pre) / math.sqrt(2.0 * math.pi)
    return cumulative + pre * density

def reference(fields, cotangent, spectral_weight, local_weight, bias_term):
    forward_factor = 1.0 / math.sqrt(NX * NY * NZ)
    inverse_factor = 1.0 / math.sqrt(KX * KY * KZ)
    outputs = []
    gradients = []
    grad_total = jnp.zeros(spectral_weight.shape, jnp.float32)
    for sample in range(N_PAIR):
        field_in = fields[sample]
        spectrum = forward_transform(field_in, forward_factor)
        mixed = mix_modes(spectrum, spectral_weight)
        spatial = inverse_transform(mixed, inverse_factor)
        pointwise = channel_mix(jnp.transpose(local_weight), field_in)
        pre = spatial + pointwise + bias_term[:, None, None, None]
        outputs.append(jax.nn.gelu(pre, approximate=False).astype(jnp.bfloat16))
        grad_pre = (cotangent[sample].astype(jnp.float32) * gelu_slope(pre)).astype(jnp.bfloat16)
        grad_spec = forward_transform(grad_pre, inverse_factor)
        grad_total = grad_total + weight_term(spectrum, grad_spec)
        grad_modes = mix_back(grad_spec, spectral_weight)
        back_spatial = inverse_transform(grad_modes, forward_factor)
        local_back = channel_mix(local_weight, grad_pre)
        gradients.append((local_back + back_spatial).astype(jnp.bfloat16))
    return (jnp.stack(outputs), jnp.stack(gradients), grad_total)
```

```python
import math

import jax
import jax.numpy as jnp
from jax import lax
from jax.sharding import PartitionSpec as P

KX = 16
KY = 16
KZ = 16


HIGHEST = lax.Precision.HIGHEST


def angle_table(modes_count, first_cell, cell_count, length):
    cells = first_cell + jnp.arange(cell_count, dtype=jnp.int32)
    waves = jnp.arange(modes_count, dtype=jnp.int32)
    phases = cells[:, None] * waves[None, :] % length
    return phases.astype(jnp.float32) * (2.0 * math.pi / length)


def turn_modes(values, cosine_table, sine_table, formula):
    half_width = values.shape[-1] // 2
    real_part = values[..., :half_width]
    imag_part = values[..., half_width:]

    def contract(operand, table):
        return jnp.einsum(formula, operand, table, precision=HIGHEST)

    first = contract(real_part, cosine_table) + contract(imag_part, sine_table)
    second = contract(imag_part, cosine_table) - contract(real_part, sine_table)
    return jnp.concatenate([first, second], axis=-1)


def depth_section(field_in):
    chans, width_x, width_y, depth = field_in.shape
    angles = angle_table(KZ, 0, depth, depth)
    table = jnp.stack([jnp.cos(angles), -jnp.sin(angles)], axis=1).astype(jnp.bfloat16)
    flat = jnp.dot(
        field_in.reshape(chans * width_x * width_y, depth),
        table.reshape(depth, 2 * KZ),
        preferred_element_type=jnp.float32,
    )
    sectioned = jnp.transpose(flat.reshape(chans, width_x, width_y, 2, KZ), (1, 2, 4, 3, 0))
    return sectioned.reshape(width_x, width_y, KZ, 2 * chans)


def channel_mix(matrix, field_in):
    chans = field_in.shape[0]
    flat = jnp.dot(matrix, field_in.reshape(chans, -1), preferred_element_type=jnp.float32)
    return flat.reshape(field_in.shape)


def depth_back(values, formula, depth):
    half_width = values.shape[-1] // 2
    angles = angle_table(KZ, 0, depth, depth)
    real_out = jnp.einsum(formula, values[..., :half_width], jnp.cos(angles), precision=HIGHEST)
    imag_out = jnp.einsum(formula, values[..., half_width:], jnp.sin(angles), precision=HIGHEST)
    return real_out - imag_out


def forward_transform(field_in, factor):
    width_x = field_in.shape[1]
    width_y = field_in.shape[2]
    total_x = width_x * lax.axis_size("px")
    total_y = width_y * lax.axis_size("py")
    sectioned = depth_section(field_in)
    sectioned = lax.all_to_all(sectioned, "py", split_axis=2, concat_axis=1, tiled=True)
    y_angles = angle_table(KY, 0, total_y, total_y)
    sectioned = turn_modes(sectioned, jnp.cos(y_angles), jnp.sin(y_angles), "xyzc,yk->xkzc")
    sectioned = lax.all_to_all(sectioned, "px", split_axis=1, concat_axis=0, tiled=True)
    x_angles = angle_table(KX, 0, total_x, total_x)
    spectrum = turn_modes(sectioned, jnp.cos(x_angles), jnp.sin(x_angles), "xyzc,xj->yzjc")
    return spectrum * factor


def inverse_transform(spectrum, factor, width_x, width_y, depth):
    total_x = width_x * lax.axis_size("px")
    total_y = width_y * lax.axis_size("py")
    x_angles = angle_table(KX, 0, total_x, total_x)
    wide = turn_modes(spectrum, jnp.cos(x_angles), -jnp.sin(x_angles), "abjc,xj->xabc")
    wide = lax.all_to_all(wide, "px", split_axis=0, concat_axis=1, tiled=True)
    y_angles = angle_table(KY, 0, total_y, total_y)
    wide = turn_modes(wide, jnp.cos(y_angles), -jnp.sin(y_angles), "xkbc,yk->xybc")
    wide = lax.all_to_all(wide, "py", split_axis=1, concat_axis=2, tiled=True)
    return depth_back(wide, "xykc,zk->cxyz", depth) * factor


def mix_modes(spectrum, weight):
    half_width = spectrum.shape[-1] // 2
    weight_full = weight.astype(jnp.float32)
    rotated = jnp.concatenate(
        [-weight_full[..., half_width:], weight_full[..., :half_width]], axis=-1
    )
    first = jnp.einsum(
        "...c,...cd->...d", spectrum[..., :half_width], weight_full, precision=HIGHEST
    )
    return first + jnp.einsum(
        "...c,...cd->...d", spectrum[..., half_width:], rotated, precision=HIGHEST
    )


def mix_back(grad_spec, weight):
    half_width = grad_spec.shape[-1] // 2
    weight_full = weight.astype(jnp.float32)
    turned = jnp.concatenate([grad_spec[..., half_width:], -grad_spec[..., :half_width]], axis=-1)
    real_out = jnp.einsum("...d,...cd->...c", grad_spec, weight_full, precision=HIGHEST)
    imag_out = jnp.einsum("...d,...cd->...c", turned, weight_full, precision=HIGHEST)
    return jnp.concatenate([real_out, imag_out], axis=-1)


def weight_term(spectrum, grad_spec):
    half_width = spectrum.shape[-1] // 2
    turned = jnp.concatenate([grad_spec[..., half_width:], -grad_spec[..., :half_width]], axis=-1)
    first = jnp.einsum("...c,...d->...cd", spectrum[..., :half_width], grad_spec, precision=HIGHEST)
    return first + jnp.einsum(
        "...c,...d->...cd", spectrum[..., half_width:], turned, precision=HIGHEST
    )


def gelu_slope(pre):
    cumulative = 0.5 * (1.0 + lax.erf(pre / math.sqrt(2.0)))
    density = jnp.exp(-0.5 * pre * pre) / math.sqrt(2.0 * math.pi)
    return cumulative + pre * density


def shards(fields, cotangent, spectral_weight, local_weight, bias_term):
    field_in = fields[0]
    width_x = field_in.shape[1]
    width_y = field_in.shape[2]
    depth = field_in.shape[3]
    total_cells = width_x * lax.axis_size("px") * width_y * lax.axis_size("py") * depth
    forward_factor = 1.0 / math.sqrt(total_cells)
    inverse_factor = 1.0 / math.sqrt(KX * KY * KZ)
    spectrum = forward_transform(field_in, forward_factor)
    mixed = mix_modes(spectrum, spectral_weight)
    spatial = inverse_transform(mixed, inverse_factor, width_x, width_y, depth)
    pointwise = channel_mix(jnp.transpose(local_weight), field_in)
    pre = spatial + pointwise + bias_term[:, None, None, None]
    activation = jax.nn.gelu(pre, approximate=False).astype(jnp.bfloat16)
    grad_pre = (cotangent[0].astype(jnp.float32) * gelu_slope(pre)).astype(jnp.bfloat16)
    grad_spec = forward_transform(grad_pre, inverse_factor)
    swap = [(0, 1), (1, 0)]
    other_spectrum = lax.ppermute(spectrum, "pair", swap)
    other_grad_spec = lax.ppermute(grad_spec, "pair", swap)
    grad_total = weight_term(spectrum, grad_spec) + weight_term(other_spectrum, other_grad_spec)
    grad_modes = mix_back(grad_spec, spectral_weight)
    back_spatial = inverse_transform(grad_modes, forward_factor, width_x, width_y, depth)
    local_back = channel_mix(local_weight, grad_pre)
    input_grad = (local_back + back_spatial).astype(jnp.bfloat16)
    return (activation[None], input_grad[None], grad_total)


def solution(mesh):
    placed = (
        P("pair", None, "px", "py", None),
        P("pair", None, "px", "py", None),
        P("px", "py", None, None, None),
        P(),
        P(),
    )
    return jax.shard_map(
        shards,
        mesh=mesh,
        in_specs=placed,
        out_specs=(
            P("pair", None, "px", "py", None),
            P("pair", None, "px", "py", None),
            P("px", "py", None, None, None),
        ),
        check_vma=False,
    )
```

```python
import math

import jax
import jax.numpy as jnp
import ml_dtypes
import numpy as np
from jax import lax
from jax.experimental import pallas as pl
from jax.experimental.pallas import tpu as pltpu
from jax.sharding import PartitionSpec as P

C = 64
KX = 16
KY = 16
KZ = 16
NX = 64
NY = 64
NZ = 128
PX = 16
PY = 8
CELLS = 32
MODES = 32
FORWARD_FACTOR = 1.0 / math.sqrt(NX * NY * NZ)
INVERSE_FACTOR = 1.0 / math.sqrt(KX * KY * KZ)
F32 = jnp.float32
BF16 = jnp.bfloat16


def cos_sin(cells, modes, length):
    phases = np.outer(np.arange(cells), np.arange(modes)) % length
    angles = phases * (2.0 * math.pi / length)
    return np.cos(angles), np.sin(angles)


def halves(table):
    table = table.astype(np.float32)
    high = table.astype(ml_dtypes.bfloat16)
    low = (table - high.astype(np.float32)).astype(ml_dtypes.bfloat16)
    return high, low


def stacked_table(table, axis):
    high, low = halves(table)
    return np.concatenate([high, high, low], axis=axis)


def depth_tables():
    cosine, sine = cos_sin(NZ, KZ, NZ)
    order = np.arange(KZ).reshape(PY, KZ // PY).T.reshape(-1)
    forward = np.concatenate([cosine.T[order], -sine.T[order]], axis=0)
    backward = np.concatenate([cosine.T[order], -sine.T[order]], axis=0)
    forward = forward.astype(np.float32).astype(ml_dtypes.bfloat16)
    return forward, stacked_table(backward, 0)


def second_tables():
    cosine, sine = cos_sin(NY, KY, NY)
    forward = np.concatenate([cosine.T, sine.T], axis=0)
    backward = np.concatenate([cosine, sine], axis=1)
    return stacked_table(forward, 1), stacked_table(backward, 1)


def first_tables():
    cosine, sine = cos_sin(NX, KX, NX)
    by_x = [cosine.reshape(PX, 2, 2, KX), sine.reshape(PX, 2, 2, KX)]
    table = np.zeros((2, 2, 2, KX, PX, 2, 2, 2))
    for kz in range(2):
        turned = [np.transpose(t, (2, 3, 0, 1)) for t in by_x]
        table[:, 0, kz, :, :, 0, kz, :] = turned[0]
        table[:, 0, kz, :, :, 1, kz, :] = turned[1]
        table[:, 1, kz, :, :, 0, kz, :] = -turned[1]
        table[:, 1, kz, :, :, 1, kz, :] = turned[0]
    table = table.reshape(128, 128)
    return stacked_table(table, 1), stacked_table(table.T, 1)


def stacked(values):
    high = values.astype(BF16)
    low = (values - high.astype(F32)).astype(BF16)
    return jnp.concatenate([high, low, high], axis=0)


def dot(left, right):
    return jnp.dot(left, right, preferred_element_type=F32)


def dot_lanes(left, right):
    return lax.dot_general(left, right, (((1,), (1,)), ((), ())), preferred_element_type=F32)


def dot_rows(left, right, precision=None):
    return lax.dot_general(
        left, right, (((0,), (0,)), ((), ())), preferred_element_type=F32, precision=precision
    )


def call(body, outs, name, scratch=(), flops=0, nbytes=0):
    return pl.pallas_call(
        body,
        out_shape=outs,
        scratch_shapes=list(scratch),
        compiler_params=pltpu.CompilerParams(vmem_limit_bytes=24 * 1024 * 1024),
        cost_estimate=pl.CostEstimate(flops=flops, bytes_accessed=nbytes, transcendentals=0),
        name=name,
    )


def shape(rows, dtype=F32, lanes=128):
    return jax.ShapeDtypeStruct((rows, lanes), dtype)


def cell_pair(wide, y, pair):
    parts = [wide[pl.ds((2 * pair + q) * 8 + y, C, stride=CELLS), :] for q in range(2)]
    return jnp.concatenate(parts, axis=0)


def put_cell_pair(wide, y, pair, values):
    for q in range(2):
        wide[pl.ds((2 * pair + q) * 8 + y, C, stride=CELLS), :] = values[q * C : (q + 1) * C]


def pair_rows(y, pair):
    return pl.ds(pl.multiple_of((y * 2 + pair) * 128, 128), 128)


def send_depth(table, cells, out_ref, y, pair):
    modes = dot_lanes(table, cells)
    for g in range(4):
        out_ref[pl.ds((g * 2 + pair) * 8 + y, PY, stride=64), :] = modes[g * 8 : (g + 1) * 8]


def depth_modes(ref, y, pair):
    parts = [ref[pl.ds((g * 2 + pair) * 8 + y, PY, stride=64), :] for g in range(4)]
    return jnp.concatenate(parts, axis=0)


def depth_body(fields_ref, table_ref, pairs_ref, out_ref, wide):
    wide[...] = fields_ref[...].astype(F32)
    table = table_ref[...]

    def step(y, carry):
        for pair in range(2):
            cells = cell_pair(wide, y, pair).astype(BF16)
            pairs_ref[pair_rows(y, pair), :] = cells
            send_depth(table, cells, out_ref, y, pair)
        return carry

    lax.fori_loop(0, 8, step, 0)


def local_body(pairs_ref, cotangent_ref, weight_ref, bias_ref, local_ref, cot_ref, wide):
    wide[...] = cotangent_ref[...].astype(F32)
    weight = weight_ref[...]
    bias = bias_ref[...]

    def step(y, carry):
        for pair in range(2):
            rows = pair_rows(y, pair)
            cells = pairs_ref[rows, :]
            both = [dot(weight, cells[q * C : (q + 1) * C]) + bias for q in range(2)]
            local_ref[rows, :] = jnp.concatenate(both, axis=0)
            cot_ref[rows, :] = cell_pair(wide, y, pair).astype(BF16)
        return carry

    lax.fori_loop(0, 8, step, 0)


def second_forward_body(in_ref, table_ref, out_ref):
    table = table_ref[...]
    turned = []
    for lb in range(8):
        column = in_ref[:, lb * 8 : (lb + 1) * 8, :].reshape(NY, 128)
        turned.append(dot(table, stacked(column)))
    for lb in range(4):
        real, imag = turned[lb], turned[lb + 4]
        out_ref[pl.ds(lb, KY, stride=8), :] = real[:KY] + imag[KY:]
        out_ref[pl.ds(lb + 4, KY, stride=8), :] = imag[:KY] - real[KY:]


def second_inverse_body(in_ref, table_ref, out_ref):
    table = table_ref[...]
    columns = [in_ref[pl.ds(lb, KY, stride=8), :] for lb in range(8)]
    for lb in range(4):
        real, imag = columns[lb], columns[lb + 4]
        one = dot(table, stacked(jnp.concatenate([real, -imag], axis=0)))
        two = dot(table, stacked(jnp.concatenate([imag, real], axis=0)))
        out_ref[:, lb * 8 : (lb + 1) * 8, :] = one.reshape(PY, 8, 128)
        out_ref[:, (lb + 4) * 8 : (lb + 5) * 8, :] = two.reshape(PY, 8, 128)


def low_lanes(values):
    lane = lax.broadcasted_iota(jnp.int32, values.shape, 1)
    return jnp.where(lane < C, values, 0.0)


def swap_lanes(values):
    return pltpu.roll(values, C, 1)


def first_forward(values, table, factor):
    spread = dot(table, stacked(values))
    spectrum = spread[:64] + swap_lanes(spread[64:])
    return low_lanes(spectrum * factor)


def first_inverse(modes, table):
    low = low_lanes(modes)
    return dot(table, stacked(jnp.concatenate([low, swap_lanes(low)], axis=0)))


def put_rows(rows_ref, index, values):
    rows_ref[pl.ds(index, MODES, stride=8), :] = values


def get_rows(rows_ref, index):
    return rows_ref[pl.ds(index, MODES, stride=8), :]


def put_halves(rows_ref, real, imag):
    for index, values in enumerate((real, imag)):
        high = values.astype(BF16).astype(F32)
        put_rows(rows_ref, index, high)
        put_rows(rows_ref, index + 2, values - high)


def mix_body(in_ref, weight_ref, table_ref, back_ref, out_ref, spectrum_ref, rows_ref, mixed_ref):
    spectrum = first_forward(in_ref[...], table_ref[...], FORWARD_FACTOR)
    spectrum_ref[...] = spectrum
    rows_ref[...] = jnp.zeros_like(rows_ref)
    put_halves(rows_ref, spectrum[:MODES], spectrum[MODES:])
    for m in range(MODES):
        rows = rows_ref[m * 8 : (m + 1) * 8, :].astype(BF16)
        mixed_ref[m * 8 : (m + 1) * 8, :] = dot(rows[:, :C], weight_ref[m * C : (m + 1) * C, :])
    by_real = get_rows(mixed_ref, 0) + get_rows(mixed_ref, 2)
    by_imag = get_rows(mixed_ref, 1) + get_rows(mixed_ref, 3)
    mixed = jnp.concatenate(
        [by_real - swap_lanes(by_imag), swap_lanes(by_real) + by_imag], axis=0
    )
    out_ref[...] = first_inverse(mixed * INVERSE_FACTOR, back_ref[...])


def both_columns(spectrum):
    real, imag = spectrum[:MODES], spectrum[MODES:]
    return real + swap_lanes(imag), imag - swap_lanes(real)


def mix_back_body(
    in_ref, weight_ref, spectrum_ref, table_ref, back_ref, out_ref, pack_ref, rows_ref, mixed_ref
):
    grad_spec = first_forward(in_ref[...], table_ref[...], INVERSE_FACTOR)
    pack_ref[0:64, :] = spectrum_ref[...]
    pack_ref[64:128, :] = grad_spec
    straight, turned = both_columns(grad_spec)
    rows_ref[...] = jnp.zeros_like(rows_ref)
    put_halves(rows_ref, straight, turned)
    mixed_ref[...] = jnp.zeros_like(mixed_ref)
    for m in range(MODES):
        rows = rows_ref[m * 8 : (m + 1) * 8, :].astype(BF16)
        mixed_ref[m * 8 : (m + 1) * 8, :C] = dot_lanes(rows, weight_ref[m * C : (m + 1) * C, :])
    real = get_rows(mixed_ref, 0) + get_rows(mixed_ref, 2)
    imag = get_rows(mixed_ref, 1) + get_rows(mixed_ref, 3)
    modes = jnp.concatenate([real, imag], axis=0)
    out_ref[...] = first_inverse(modes * FORWARD_FACTOR, back_ref[...])


def weight_grad_body(mine_ref, other_ref, out_ref, left_ref, right_ref):
    left_ref[...] = jnp.zeros_like(left_ref)
    right_ref[...] = jnp.zeros_like(right_ref)
    for index, pack_ref in enumerate((mine_ref, other_ref)):
        straight, turned = both_columns(pack_ref[64:128, :])
        put_rows(left_ref, 2 * index, pack_ref[0:MODES, :])
        put_rows(left_ref, 2 * index + 1, pack_ref[MODES : 2 * MODES, :])
        put_rows(right_ref, 2 * index, straight)
        put_rows(right_ref, 2 * index + 1, turned)
    for m in range(MODES):
        rows = slice(m * 8, (m + 1) * 8)
        out_ref[m * C : (m + 1) * C, :] = dot_rows(
            left_ref[rows, :], right_ref[rows, :], lax.Precision.HIGHEST
        )[:C]


ERFC = (
    0.17087277,
    -0.82215223,
    1.48851587,
    -1.13520398,
    0.27886807,
    -0.18628806,
    0.09678418,
    0.37409196,
    1.00002368,
    -1.26551223,
)


def gelu_and_slope(pre):
    bell = jnp.exp(-0.5 * pre * pre)
    t = 1.0 / (1.0 + (0.5 / math.sqrt(2.0)) * jnp.abs(pre))
    series = jnp.full_like(t, ERFC[0])
    for coefficient in ERFC[1:]:
        series = series * t + coefficient
    tail = (0.5 * t) * (jnp.exp(series) * bell)
    cumulative = jnp.where(pre < 0.0, tail, 1.0 - tail)
    return pre * cumulative, cumulative + pre * (bell * (1.0 / math.sqrt(2.0 * math.pi)))


def middle_body(
    in_ref, local_ref, cot_ref, back_ref, table_ref, act_ref, grad_ref, out_ref, wide
):
    back = back_ref[...]
    table = table_ref[...]

    def step(y, carry):
        for pair in range(2):
            rows = pair_rows(y, pair)
            pre = local_ref[rows, :] + dot_rows(stacked(depth_modes(in_ref, y, pair)), back)
            activation, slope = gelu_and_slope(pre)
            put_cell_pair(wide, y, pair, activation)
            grad_pre = (cot_ref[rows, :].astype(F32) * slope).astype(BF16)
            grad_ref[rows, :] = grad_pre
            send_depth(table, grad_pre, out_ref, y, pair)
        return carry

    lax.fori_loop(0, 8, step, 0)
    act_ref[...] = wide[...].astype(BF16)


def last_body(in_ref, grad_ref, weight_ref, back_ref, out_ref, wide):
    back = back_ref[...]
    weight = weight_ref[...]

    def step(y, carry):
        for pair in range(2):
            cells = grad_ref[pair_rows(y, pair), :]
            both = [dot(weight, cells[q * C : (q + 1) * C]) for q in range(2)]
            total = jnp.concatenate(both, axis=0)
            total += dot_rows(stacked(depth_modes(in_ref, y, pair)), back)
            put_cell_pair(wide, y, pair, total)
        return carry

    lax.fori_loop(0, 8, step, 0)
    out_ref[...] = wide[...].astype(BF16)


def over_py(values):
    return lax.all_to_all(values.reshape(PY, 64, 128), "py", 0, 0, tiled=True)


def over_px(values):
    return lax.all_to_all(values.reshape(PX, 8, 128), "px", 0, 0, tiled=True).reshape(128, 128)


def shards(fields, cotangent, spectral_weight, local_weight, bias_term):
    depth_table, depth_back = depth_tables()
    second_table, second_back = second_tables()
    first_table, first_back = first_tables()
    weight = spectral_weight.reshape(MODES * C, 128)
    wide = pltpu.VMEM((C * CELLS, 128), F32)
    rows = pltpu.VMEM((MODES * 8, 128), F32)
    cells = C * CELLS
    second_forward = call(second_forward_body, shape(128), "y_forward")
    second_inverse = call(
        second_inverse_body, jax.ShapeDtypeStruct((PY, 64, 128), F32), "y_inverse"
    )

    pairs, sent = call(depth_body, (shape(cells, BF16), shape(512)), "z_forward", [wide])(
        fields.reshape(cells, 128), depth_table
    )
    received = over_py(sent)
    local, cot = call(
        local_body,
        (shape(cells), shape(cells, BF16)),
        "local_mix",
        [wide],
        flops=2 * C * cells * 128,
        nbytes=5 * cells * 256,
    )(
        pairs,
        cotangent.reshape(cells, 128),
        jnp.transpose(local_weight),
        bias_term.reshape(C, 1),
    )
    received = over_px(second_forward(received, second_table))
    sent, spectrum = call(mix_body, (shape(128), shape(64)), "modes_mix", [rows, rows])(
        received, weight, first_table, first_back
    )
    received = over_py(second_inverse(over_px(sent), second_back))
    activation, grad_pre, sent = call(
        middle_body,
        (shape(cells, BF16), shape(cells, BF16), shape(512)),
        "gelu_z",
        [wide],
    )(received.reshape(512, 128), local, cot, depth_back, depth_table)
    received = over_px(second_forward(over_py(sent), second_table))
    sent, pack = call(mix_back_body, (shape(128), shape(128)), "modes_back", [rows, rows])(
        received, weight, spectrum, first_table, first_back
    )
    received = over_px(sent)
    other = lax.ppermute(pack, "pair", [(0, 1), (1, 0)])
    weight_grad = call(
        weight_grad_body, shape(MODES * C), "weight_grad", [rows, rows], flops=10**8, nbytes=10**6
    )(pack, other)
    received = over_py(second_inverse(received, second_back))
    input_grad = call(last_body, shape(cells, BF16), "z_inverse", [wide])(
        received.reshape(512, 128), grad_pre, local_weight, depth_back
    )
    return (
        activation.reshape(fields.shape),
        input_grad.reshape(fields.shape),
        weight_grad.reshape(spectral_weight.shape),
    )


def solution(mesh):
    grid = P("pair", None, "px", "py", None)
    modes = P("px", "py", None, None, None)
    return jax.shard_map(
        shards,
        mesh=mesh,
        in_specs=(grid, grid, modes, P(), P()),
        out_specs=(grid, grid, modes),
        check_vma=False,
    )
```

```python
import math

import jax
import jax.numpy as jnp
import ml_dtypes
import numpy as np
from jax import lax
from jax.experimental import pallas as pl
from jax.experimental.pallas import tpu as pltpu
from jax.sharding import PartitionSpec as P

C = 64
KX = 16
KY = 16
KZ = 16
NX = 64
NY = 64
NZ = 128
PX = 16
PY = 8
CELLS = 32
MODES = 32
FORWARD_FACTOR = 1.0 / math.sqrt(NX * NY * NZ)
INVERSE_FACTOR = 1.0 / math.sqrt(KX * KY * KZ)
F32 = jnp.float32
BF16 = jnp.bfloat16
MIDDLE_GROUP = 1
LAST_GROUP = 1


def cos_sin(cells, modes, length):
    phases = np.outer(np.arange(cells), np.arange(modes)) % length
    angles = phases * (2.0 * math.pi / length)
    return np.cos(angles), np.sin(angles)


def halves(table):
    table = table.astype(np.float32)
    high = table.astype(ml_dtypes.bfloat16)
    low = (table - high.astype(np.float32)).astype(ml_dtypes.bfloat16)
    return high, low


def stacked_table(table, axis):
    high, low = halves(table)
    return np.concatenate([high, high, low], axis=axis)


def depth_tables():
    cosine, sine = cos_sin(NZ, KZ, NZ)
    order = np.arange(KZ).reshape(PY, KZ // PY).T.reshape(-1)
    forward = np.concatenate([cosine.T[order], -sine.T[order]], axis=0)
    backward = np.concatenate([cosine.T[order], -sine.T[order]], axis=0)
    forward = forward.astype(np.float32).astype(ml_dtypes.bfloat16)
    return forward, stacked_table(backward, 0)


def second_tables():
    cosine, sine = cos_sin(NY, KY, NY)
    forward = np.concatenate([cosine.T, sine.T], axis=0)
    backward = np.concatenate([cosine, sine], axis=1)
    return stacked_table(forward, 1), stacked_table(backward, 1)


def first_tables():
    cosine, sine = cos_sin(NX, KX, NX)
    by_x = [cosine.reshape(PX, 2, 2, KX), sine.reshape(PX, 2, 2, KX)]
    table = np.zeros((2, 2, 2, KX, PX, 2, 2, 2))
    for kz in range(2):
        turned = [np.transpose(t, (2, 3, 0, 1)) for t in by_x]
        table[:, 0, kz, :, :, 0, kz, :] = turned[0]
        table[:, 0, kz, :, :, 1, kz, :] = turned[1]
        table[:, 1, kz, :, :, 0, kz, :] = -turned[1]
        table[:, 1, kz, :, :, 1, kz, :] = turned[0]
    table = table.reshape(128, 128)
    return stacked_table(table, 1), stacked_table(table.T, 1)


def small_tables():
    pieces = depth_tables() + second_tables()
    rows = [np.pad(p, ((0, 0), (0, 256 - p.shape[1]))) for p in pieces]
    return np.concatenate(rows, axis=0)


DEPTH = (slice(0, 32), slice(0, 128))
DEPTH_BACK = (slice(32, 128), slice(0, 128))
SECOND = (slice(128, 160), slice(0, 192))
SECOND_BACK = (slice(160, 224), slice(0, 96))


def stacked(values):
    high = values.astype(BF16)
    low = (values - high.astype(F32)).astype(BF16)
    return jnp.concatenate([high, low, high], axis=0)


def dot(left, right):
    return jnp.dot(left, right, preferred_element_type=F32)


def dot_lanes(left, right):
    return lax.dot_general(left, right, (((1,), (1,)), ((), ())), preferred_element_type=F32)


def dot_rows(left, right, precision=None):
    return lax.dot_general(
        left, right, (((0,), (0,)), ((), ())), preferred_element_type=F32, precision=precision
    )


def call(body, outs, name, scratch=(), flops=0, nbytes=0, **specs):
    return pl.pallas_call(
        body,
        out_shape=outs,
        scratch_shapes=list(scratch),
        compiler_params=pltpu.CompilerParams(vmem_limit_bytes=24 * 1024 * 1024),
        cost_estimate=pl.CostEstimate(flops=flops, bytes_accessed=nbytes, transcendentals=0),
        name=name,
        **specs,
    )


def shape(rows, dtype=F32, lanes=128):
    return jax.ShapeDtypeStruct((rows, lanes), dtype)


def cell_pair(wide, y):
    parts = [wide[pl.ds(q * 8 + y, C, stride=16), :] for q in range(2)]
    return jnp.concatenate(parts, axis=0)


def put_cell_pair(wide, y, values):
    for q in range(2):
        wide[pl.ds(q * 8 + y, C, stride=16), :] = values[q * C : (q + 1) * C]


def block(y, pair):
    return slice(pair * 128, (pair + 1) * 128), slice(y * 128, (y + 1) * 128)


def send_depth(table, cells, out_ref, ys, pair):
    modes = dot_lanes(table, cells)
    for i, y in enumerate(ys):
        for g in range(4):
            out_ref[pl.ds((g * 2 + pair) * 8 + y, PY, stride=64), :] = modes[
                g * 8 : (g + 1) * 8, i * 128 : (i + 1) * 128
            ]


def depth_modes(ref, ys, pair):
    def one(y, g):
        return ref[pl.ds((g * 2 + pair) * 8 + y, PY, stride=64), :]

    return jnp.concatenate(
        [jnp.concatenate([one(y, g) for y in ys], axis=1) for g in range(4)], axis=0
    )


def back_and_local(in_ref, back, weight, cells_ref, ys, pair):
    total = dot_rows(stacked(depth_modes(in_ref, ys, pair)), back)
    rows = slice(pair * 128, (pair + 1) * 128)
    mixed = dot(weight, cells_ref[rows, ys[0] * 128 : (ys[-1] + 1) * 128])
    parts = [mixed[:, i * 128 : (i + 1) * 128] for i in range(len(ys))]
    return total + jnp.concatenate(parts, axis=0)


def both_cells(weight):
    zero = jnp.zeros_like(weight)
    return jnp.concatenate(
        [jnp.concatenate([weight, zero], axis=1), jnp.concatenate([zero, weight], axis=1)], axis=0
    ).astype(BF16)


def y_groups(size):
    return [list(range(first, first + size)) for first in range(0, 8, size)]


def part_of(ref, pair):
    return ref.at[:, pl.ds(pair * 16, 16), :]


def depth_table_here():
    row = lax.broadcasted_iota(jnp.int32, (32, 128), 0)
    cell = lax.broadcasted_iota(jnp.int32, (32, 128), 1)
    wave = 2 * (row % 8) + (row // 8) % 2
    phase = (wave * cell + (NZ // 4) * (row // 16)) % NZ
    return jnp.cos(phase.astype(F32) * (2.0 * math.pi / NZ)).astype(BF16)


def depth_body(fields_ref, pairs_ref, out_ref, wide):
    table = depth_table_here()
    for pair in range(2):
        part = fields_ref[:, pair * 16 : (pair + 1) * 16, :]
        wide[...] = part.astype(F32).reshape(C * 16, 128)
        for y in range(8):
            cells = cell_pair(wide, y).astype(BF16)
            pairs_ref[block(y, pair)] = cells
            send_depth(table, cells, out_ref, [y], pair)


def second_forward_body(in_ref, table_ref, out_ref):
    table = table_ref[SECOND]
    turned = []
    for lb in range(8):
        column = in_ref[:, lb * 8 : (lb + 1) * 8, :].reshape(NY, 128)
        turned.append(dot(table, stacked(column)))
    for lb in range(4):
        real, imag = turned[lb], turned[lb + 4]
        out_ref[pl.ds(lb, KY, stride=8), :] = real[:KY] + imag[KY:]
        out_ref[pl.ds(lb + 4, KY, stride=8), :] = imag[:KY] - real[KY:]


def second_inverse_body(in_ref, table_ref, out_ref):
    table = table_ref[SECOND_BACK]
    columns = [in_ref[pl.ds(lb, KY, stride=8), :] for lb in range(8)]
    for lb in range(4):
        real, imag = columns[lb], columns[lb + 4]
        one = dot(table, stacked(jnp.concatenate([real, -imag], axis=0)))
        two = dot(table, stacked(jnp.concatenate([imag, real], axis=0)))
        out_ref[:, lb * 8 : (lb + 1) * 8, :] = one.reshape(PY, 8, 128)
        out_ref[:, (lb + 4) * 8 : (lb + 5) * 8, :] = two.reshape(PY, 8, 128)


def low_lanes(values):
    lane = lax.broadcasted_iota(jnp.int32, values.shape, 1)
    return jnp.where(lane < C, values, 0.0)


def swap_lanes(values):
    return pltpu.roll(values, C, 1)


def first_forward(values, table, factor):
    spread = dot(table, stacked(values))
    spectrum = spread[:64] + swap_lanes(spread[64:])
    return low_lanes(spectrum * factor)


def first_inverse(modes, table):
    low = low_lanes(modes)
    return dot(table, stacked(jnp.concatenate([low, swap_lanes(low)], axis=0)))


def put_rows(rows_ref, index, values):
    rows_ref[pl.ds(index, MODES, stride=8), :] = values


def get_rows(rows_ref, index):
    return rows_ref[pl.ds(index, MODES, stride=8), :]


def put_halves(rows_ref, real, imag):
    for index, values in enumerate((real, imag)):
        high = values.astype(BF16).astype(F32)
        put_rows(rows_ref, index, high)
        put_rows(rows_ref, index + 2, values - high)


def mix_body(
    in_ref, weight_ref, table_ref, back_ref, local_ref, bias_ref,
    out_ref, spectrum_ref, turned_ref, column_ref, rows_ref, mixed_ref,
):
    turned_ref[...] = both_cells(jnp.transpose(local_ref[...].astype(F32)))
    bias = jnp.transpose(jnp.broadcast_to(bias_ref[...], (128, C)))
    column_ref[...] = jnp.concatenate([bias, bias], axis=0)
    spectrum = first_forward(in_ref[...], table_ref[...], FORWARD_FACTOR)
    spectrum_ref[...] = spectrum
    rows_ref[...] = jnp.zeros_like(rows_ref)
    put_halves(rows_ref, spectrum[:MODES], spectrum[MODES:])
    for m in range(MODES):
        rows = rows_ref[m * 8 : (m + 1) * 8, :].astype(BF16)
        mixed_ref[m * 8 : (m + 1) * 8, :] = dot(rows[:, :C], weight_ref[m * C : (m + 1) * C, :])
    by_real = get_rows(mixed_ref, 0) + get_rows(mixed_ref, 2)
    by_imag = get_rows(mixed_ref, 1) + get_rows(mixed_ref, 3)
    mixed = jnp.concatenate(
        [by_real - swap_lanes(by_imag), swap_lanes(by_real) + by_imag], axis=0
    )
    out_ref[...] = first_inverse(mixed * INVERSE_FACTOR, back_ref[...])


def both_columns(spectrum):
    real, imag = spectrum[:MODES], spectrum[MODES:]
    return real + swap_lanes(imag), imag - swap_lanes(real)


def mix_back_body(
    in_ref, weight_ref, spectrum_ref, table_ref, back_ref, out_ref, pack_ref, rows_ref, mixed_ref
):
    grad_spec = first_forward(in_ref[...], table_ref[...], INVERSE_FACTOR)
    pack_ref[0:64, :] = spectrum_ref[...]
    pack_ref[64:128, :] = grad_spec
    straight, turned = both_columns(grad_spec)
    rows_ref[...] = jnp.zeros_like(rows_ref)
    put_halves(rows_ref, straight, turned)
    mixed_ref[...] = jnp.zeros_like(mixed_ref)
    for m in range(MODES):
        rows = rows_ref[m * 8 : (m + 1) * 8, :].astype(BF16)
        mixed_ref[m * 8 : (m + 1) * 8, :C] = dot_lanes(rows, weight_ref[m * C : (m + 1) * C, :])
    real = get_rows(mixed_ref, 0) + get_rows(mixed_ref, 2)
    imag = get_rows(mixed_ref, 1) + get_rows(mixed_ref, 3)
    modes = jnp.concatenate([real, imag], axis=0)
    out_ref[...] = first_inverse(modes * FORWARD_FACTOR, back_ref[...])


def weight_grad_body(
    mine_ref, other_ref, pairs_ref, out_ref, act_ref, left_ref, right_ref, wide
):
    left_ref[...] = jnp.zeros_like(left_ref)
    right_ref[...] = jnp.zeros_like(right_ref)
    for index, pack_ref in enumerate((mine_ref, other_ref)):
        straight, turned = both_columns(pack_ref[64:128, :])
        put_rows(left_ref, 2 * index, pack_ref[0:MODES, :])
        put_rows(left_ref, 2 * index + 1, pack_ref[MODES : 2 * MODES, :])
        put_rows(right_ref, 2 * index, straight)
        put_rows(right_ref, 2 * index + 1, turned)
    for m in range(MODES):
        rows = slice(m * 8, (m + 1) * 8)
        out_ref[m * C : (m + 1) * C, :] = dot_rows(
            left_ref[rows, :], right_ref[rows, :], lax.Precision.HIGHEST
        )[:C]
    for pair in range(2):
        for y in range(8):
            put_cell_pair(wide, y, pairs_ref[block(y, pair)].astype(F32))
        act_ref[:, pair * 16 : (pair + 1) * 16, :] = (
            wide[...].astype(BF16).reshape(C, 16, 128)
        )


ERFC = (
    0.17087277,
    -0.82215223,
    1.48851587,
    -1.13520398,
    0.27886807,
    -0.18628806,
    0.09678418,
    0.37409196,
    1.00002368,
    -1.26551223,
)


def gelu_and_slope(pre):
    bell = jnp.exp(-0.5 * pre * pre)
    t = 1.0 / (1.0 + (0.5 / math.sqrt(2.0)) * jnp.abs(pre))
    series = jnp.full_like(t, ERFC[0])
    for coefficient in ERFC[1:]:
        series = series * t + coefficient
    tail = (0.5 * t) * (jnp.exp(series) * bell)
    cumulative = jnp.where(pre < 0.0, tail, 1.0 - tail)
    return pre * cumulative, cumulative + pre * (bell * (1.0 / math.sqrt(2.0 * math.pi)))


def middle_body(
    in_ref, pairs_ref, cotangent_ref, weight_ref, column_ref, table_ref, act_ref, grad_ref,
    out_ref, wide,
):
    weight = weight_ref[...]
    bias = jnp.concatenate([column_ref[...]] * MIDDLE_GROUP, axis=0)
    back = table_ref[DEPTH_BACK]
    table = table_ref[DEPTH]
    for pair in range(2):
        part = cotangent_ref[:, pair * 16 : (pair + 1) * 16, :]
        wide[...] = part.astype(F32).reshape(C * 16, 128)
        for ys in y_groups(MIDDLE_GROUP):
            pre = back_and_local(in_ref, back, weight, pairs_ref, ys, pair) + bias
            activation, slope = gelu_and_slope(pre)
            cotangent = jnp.concatenate([cell_pair(wide, y) for y in ys], axis=0)
            activation = activation.astype(BF16)
            grad_pre = (cotangent * slope).astype(BF16)
            send_depth(table, grad_pre, out_ref, ys, pair)
            for i, y in enumerate(ys):
                act_ref[block(y, pair)] = activation[i * 128 : (i + 1) * 128]
                grad_ref[block(y, pair)] = grad_pre[i * 128 : (i + 1) * 128]


def last_body(in_ref, grad_ref, weight_ref, table_ref, out_ref, wide, cells_ref, sems):
    back = table_ref[DEPTH_BACK]
    weight = both_cells(weight_ref[...].astype(F32))
    copies = []
    for pair in range(2):
        for ys in y_groups(LAST_GROUP):
            total = back_and_local(in_ref, back, weight, grad_ref, ys, pair)
            for i, y in enumerate(ys):
                put_cell_pair(wide, y, total[i * 128 : (i + 1) * 128])
        cells_ref[pair] = wide[...].astype(BF16).reshape(C, 16, 128)
        copies.append(
            pltpu.make_async_copy(cells_ref.at[pair], part_of(out_ref, pair), sems.at[pair])
        )
        copies[pair].start()
    for copy in copies:
        copy.wait()


def over_py(values):
    return lax.all_to_all(values.reshape(PY, 64, 128), "py", 0, 0, tiled=True)


def over_px(values):
    return lax.all_to_all(values.reshape(PX, 8, 128), "px", 0, 0, tiled=True).reshape(128, 128)


def shards(fields, cotangent, spectral_weight, local_weight, bias_term):
    small = small_tables()
    first_table, first_back = first_tables()
    weight = spectral_weight.reshape(MODES * C, 128)
    wide = pltpu.VMEM((C * 16, 128), F32)
    halves_of_cells = pltpu.VMEM((2, C, 16, 128), BF16)
    rows = pltpu.VMEM((MODES * 8, 128), F32)
    cells = C * CELLS
    grid = jax.ShapeDtypeStruct((C, CELLS, 128), BF16)
    in_place = pl.BlockSpec(memory_space=pltpu.HBM)
    second_forward = call(second_forward_body, shape(128), "y_forward")
    second_inverse = call(
        second_inverse_body, jax.ShapeDtypeStruct((PY, 64, 128), F32), "y_inverse"
    )

    pairs, sent = call(
        depth_body,
        (shape(256, BF16, 1024), shape(512)),
        "z_forward",
        [wide],
    )(fields.reshape(C, CELLS, 128))
    received = over_px(second_forward(over_py(sent), small))
    sent, spectrum, turned, column = call(
        mix_body,
        (shape(128), shape(64), shape(128, BF16), shape(128)),
        "modes_mix",
        [rows, rows],
    )(received, weight, first_table, first_back, local_weight, bias_term.reshape(1, C))
    received = over_py(second_inverse(over_px(sent), small))
    activation, grad_pre, sent = call(
        middle_body,
        (shape(256, BF16, 1024), shape(256, BF16, 1024), shape(512)),
        "gelu_z",
        [wide],
    )(
        received.reshape(512, 128),
        pairs,
        cotangent.reshape(C, CELLS, 128),
        turned,
        column,
        small,
    )
    received = over_px(second_forward(over_py(sent), small))
    sent, pack = call(mix_back_body, (shape(128), shape(128)), "modes_back", [rows, rows])(
        received, weight, spectrum, first_table, first_back
    )
    received = over_px(sent)
    other = lax.ppermute(pack, "pair", [(0, 1), (1, 0)])
    weight_grad, activation = call(
        weight_grad_body,
        (shape(MODES * C), grid),
        "weight_grad",
        [rows, rows, wide],
        flops=10**8,
        nbytes=10**6,
    )(pack, other, activation)
    received = over_py(second_inverse(received, small))
    input_grad = call(
        last_body,
        grid,
        "z_inverse",
        [wide, halves_of_cells, pltpu.SemaphoreType.DMA((2,))],
        out_specs=in_place,
    )(received.reshape(512, 128), grad_pre, local_weight, small)
    return (
        activation.reshape(fields.shape),
        input_grad.reshape(fields.shape),
        weight_grad.reshape(spectral_weight.shape),
    )


def solution(mesh):
    grid = P("pair", None, "px", "py", None)
    modes = P("px", "py", None, None, None)
    return jax.shard_map(
        shards,
        mesh=mesh,
        in_specs=(grid, grid, modes, P(), P()),
        out_specs=(grid, grid, modes),
        check_vma=False,
    )
```

```python
import math

import jax
import jax.numpy as jnp
import ml_dtypes
import numpy as np
from jax import lax
from jax.experimental import pallas as pl
from jax.experimental.pallas import tpu as pltpu
from jax.sharding import PartitionSpec as P

C = 64
KX = 16
KY = 16
KZ = 16
NX = 64
NY = 64
NZ = 128
PX = 16
PY = 8
CELLS = 32
MODES = 32
FORWARD_FACTOR = 1.0 / math.sqrt(NX * NY * NZ)
INVERSE_FACTOR = 1.0 / math.sqrt(KX * KY * KZ)
F32 = jnp.float32
BF16 = jnp.bfloat16
PY_ORDER = (0, 4, 7, 3, 1, 5, 6, 2)
MIDDLE_GROUP = 1
LAST_GROUP = 1


def cos_sin(cells, modes, length):
    phases = np.outer(np.arange(cells), np.arange(modes)) % length
    angles = phases * (2.0 * math.pi / length)
    return np.cos(angles), np.sin(angles)


def halves(table):
    table = table.astype(np.float32)
    high = table.astype(ml_dtypes.bfloat16)
    low = (table - high.astype(np.float32)).astype(ml_dtypes.bfloat16)
    return high, low


def stacked_table(table, axis):
    high, low = halves(table)
    return np.concatenate([high, high, low], axis=axis)


def depth_tables():
    cosine, sine = cos_sin(NZ, KZ, NZ)
    order = np.array([2 * peer + kz for kz in range(2) for peer in PY_ORDER])
    forward = np.concatenate([cosine.T[order], -sine.T[order]], axis=0)
    backward = np.concatenate([cosine.T[order], -sine.T[order]], axis=0)
    forward = forward.astype(np.float32).astype(ml_dtypes.bfloat16)
    return forward, stacked_table(backward, 0)


def second_tables():
    cosine, sine = cos_sin(NY, KY, NY)
    cells = np.array([8 * peer + cell for peer in PY_ORDER for cell in range(8)])
    cosine, sine = cosine[cells], sine[cells]
    forward = np.concatenate([cosine.T, sine.T], axis=0)
    backward = np.concatenate([cosine, sine], axis=1)
    return stacked_table(forward, 1), stacked_table(backward, 1)


def first_tables():
    cosine, sine = cos_sin(NX, KX, NX)
    by_x = [cosine.reshape(PX, 2, 2, KX), sine.reshape(PX, 2, 2, KX)]
    table = np.zeros((2, 2, 2, KX, PX, 2, 2, 2))
    for kz in range(2):
        turned = [np.transpose(t, (2, 3, 0, 1)) for t in by_x]
        table[:, 0, kz, :, :, 0, kz, :] = turned[0]
        table[:, 0, kz, :, :, 1, kz, :] = turned[1]
        table[:, 1, kz, :, :, 0, kz, :] = -turned[1]
        table[:, 1, kz, :, :, 1, kz, :] = turned[0]
    table = table.reshape(128, 128)
    return stacked_table(table, 1), stacked_table(table.T, 1)


def small_tables():
    pieces = depth_tables() + second_tables()
    rows = [np.pad(p, ((0, 0), (0, 256 - p.shape[1]))) for p in pieces]
    return np.concatenate(rows, axis=0)


DEPTH = (slice(0, 32), slice(0, 128))
DEPTH_BACK = (slice(32, 128), slice(0, 128))
SECOND = (slice(128, 160), slice(0, 192))
SECOND_BACK = (slice(160, 224), slice(0, 96))


def stacked(values):
    high = values.astype(BF16)
    low = (values - high.astype(F32)).astype(BF16)
    return jnp.concatenate([high, low, high], axis=0)


def dot(left, right):
    return jnp.dot(left, right, preferred_element_type=F32)


def dot_lanes(left, right):
    return lax.dot_general(left, right, (((1,), (1,)), ((), ())), preferred_element_type=F32)


def dot_rows(left, right, precision=None):
    return lax.dot_general(
        left, right, (((0,), (0,)), ((), ())), preferred_element_type=F32, precision=precision
    )


def call(body, outs, name, scratch=(), flops=0, nbytes=0, **specs):
    return pl.pallas_call(
        body,
        out_shape=outs,
        scratch_shapes=list(scratch),
        compiler_params=pltpu.CompilerParams(vmem_limit_bytes=24 * 1024 * 1024),
        cost_estimate=pl.CostEstimate(flops=flops, bytes_accessed=nbytes, transcendentals=0),
        name=name,
        **specs,
    )


def shape(rows, dtype=F32, lanes=128):
    return jax.ShapeDtypeStruct((rows, lanes), dtype)


def cell_pair(wide, y):
    parts = [wide[pl.ds(q * 8 + y, C, stride=16), :] for q in range(2)]
    return jnp.concatenate(parts, axis=0)


def put_cell_pair(wide, y, values):
    for q in range(2):
        wide[pl.ds(q * 8 + y, C, stride=16), :] = values[q * C : (q + 1) * C]


def block(y, pair):
    return slice(pair * 128, (pair + 1) * 128), slice(y * 128, (y + 1) * 128)


def send_depth(table, cells, out_ref, ys, pair):
    modes = dot_lanes(table, cells)
    for i, y in enumerate(ys):
        for g in range(4):
            out_ref[pl.ds((g * 2 + pair) * 8 + y, PY, stride=64), :] = modes[
                g * 8 : (g + 1) * 8, i * 128 : (i + 1) * 128
            ]


def depth_modes(ref, ys, pair):
    def one(y, g):
        return ref[pl.ds((g * 2 + pair) * 8 + y, PY, stride=64), :]

    return jnp.concatenate(
        [jnp.concatenate([one(y, g) for y in ys], axis=1) for g in range(4)], axis=0
    )


def back_and_local(in_ref, back, weight, cells_ref, ys, pair):
    total = dot_rows(stacked(depth_modes(in_ref, ys, pair)), back)
    rows = slice(pair * 128, (pair + 1) * 128)
    mixed = dot(weight, cells_ref[rows, ys[0] * 128 : (ys[-1] + 1) * 128])
    parts = [mixed[:, i * 128 : (i + 1) * 128] for i in range(len(ys))]
    return total + jnp.concatenate(parts, axis=0)


def both_cells(weight):
    zero = jnp.zeros_like(weight)
    return jnp.concatenate(
        [jnp.concatenate([weight, zero], axis=1), jnp.concatenate([zero, weight], axis=1)], axis=0
    ).astype(BF16)


def y_groups(size):
    return [list(range(first, first + size)) for first in range(0, 8, size)]


def part_of(ref, pair):
    return ref.at[:, pl.ds(pair * 16, 16), :]


def depth_table_here():
    row = lax.broadcasted_iota(jnp.int32, (32, 128), 0)
    cell = lax.broadcasted_iota(jnp.int32, (32, 128), 1)
    peer = sum(jnp.where(row % 8 == slot, peer, 0) for slot, peer in enumerate(PY_ORDER))
    wave = 2 * peer + (row // 8) % 2
    phase = (wave * cell + (NZ // 4) * (row // 16)) % NZ
    return jnp.cos(phase.astype(F32) * (2.0 * math.pi / NZ)).astype(BF16)


def depth_body(fields_ref, pairs_ref, out_ref, wide):
    table = depth_table_here()
    for pair in range(2):
        part = fields_ref[:, pair * 16 : (pair + 1) * 16, :]
        wide[...] = part.astype(F32).reshape(C * 16, 128)
        for y in range(8):
            cells = cell_pair(wide, y).astype(BF16)
            pairs_ref[block(y, pair)] = cells
            send_depth(table, cells, out_ref, [y], pair)


def second_forward_body(in_ref, table_ref, out_ref):
    table = table_ref[SECOND]
    turned = []
    for lb in range(8):
        column = in_ref[:, lb * 8 : (lb + 1) * 8, :].reshape(NY, 128)
        turned.append(dot(table, stacked(column)))
    for lb in range(4):
        real, imag = turned[lb], turned[lb + 4]
        out_ref[pl.ds(lb, KY, stride=8), :] = real[:KY] + imag[KY:]
        out_ref[pl.ds(lb + 4, KY, stride=8), :] = imag[:KY] - real[KY:]


def second_inverse_body(in_ref, table_ref, out_ref):
    table = table_ref[SECOND_BACK]
    columns = [in_ref[pl.ds(lb, KY, stride=8), :] for lb in range(8)]
    for lb in range(4):
        real, imag = columns[lb], columns[lb + 4]
        one = dot(table, stacked(jnp.concatenate([real, -imag], axis=0)))
        two = dot(table, stacked(jnp.concatenate([imag, real], axis=0)))
        out_ref[:, lb * 8 : (lb + 1) * 8, :] = one.reshape(PY, 8, 128)
        out_ref[:, (lb + 4) * 8 : (lb + 5) * 8, :] = two.reshape(PY, 8, 128)


def low_lanes(values):
    lane = lax.broadcasted_iota(jnp.int32, values.shape, 1)
    return jnp.where(lane < C, values, 0.0)


def swap_lanes(values):
    return pltpu.roll(values, C, 1)


def first_forward(values, table, factor):
    spread = dot(table, stacked(values))
    spectrum = spread[:64] + swap_lanes(spread[64:])
    return low_lanes(spectrum * factor)


def first_inverse(modes, table):
    low = low_lanes(modes)
    return dot(table, stacked(jnp.concatenate([low, swap_lanes(low)], axis=0)))


def put_rows(rows_ref, index, values):
    rows_ref[pl.ds(index, MODES, stride=8), :] = values


def get_rows(rows_ref, index):
    return rows_ref[pl.ds(index, MODES, stride=8), :]


def put_halves(rows_ref, real, imag):
    for index, values in enumerate((real, imag)):
        high = values.astype(BF16).astype(F32)
        put_rows(rows_ref, index, high)
        put_rows(rows_ref, index + 2, values - high)


def mix_body(
    in_ref, weight_ref, table_ref, back_ref, local_ref, bias_ref,
    out_ref, spectrum_ref, turned_ref, column_ref, rows_ref, mixed_ref,
):
    turned_ref[...] = both_cells(jnp.transpose(local_ref[...].astype(F32)))
    bias = jnp.transpose(jnp.broadcast_to(bias_ref[...], (128, C)))
    column_ref[...] = jnp.concatenate([bias, bias], axis=0)
    spectrum = first_forward(in_ref[...], table_ref[...], FORWARD_FACTOR)
    spectrum_ref[...] = spectrum
    rows_ref[...] = jnp.zeros_like(rows_ref)
    put_halves(rows_ref, spectrum[:MODES], spectrum[MODES:])
    for m in range(MODES):
        rows = rows_ref[m * 8 : (m + 1) * 8, :].astype(BF16)
        mixed_ref[m * 8 : (m + 1) * 8, :] = dot(rows[:, :C], weight_ref[m * C : (m + 1) * C, :])
    by_real = get_rows(mixed_ref, 0) + get_rows(mixed_ref, 2)
    by_imag = get_rows(mixed_ref, 1) + get_rows(mixed_ref, 3)
    mixed = jnp.concatenate(
        [by_real - swap_lanes(by_imag), swap_lanes(by_real) + by_imag], axis=0
    )
    out_ref[...] = first_inverse(mixed * INVERSE_FACTOR, back_ref[...])


def both_columns(spectrum):
    real, imag = spectrum[:MODES], spectrum[MODES:]
    return real + swap_lanes(imag), imag - swap_lanes(real)


def mix_back_body(
    in_ref, weight_ref, spectrum_ref, table_ref, back_ref, out_ref, pack_ref, rows_ref, mixed_ref
):
    grad_spec = first_forward(in_ref[...], table_ref[...], INVERSE_FACTOR)
    pack_ref[0:64, :] = spectrum_ref[...]
    pack_ref[64:128, :] = grad_spec
    straight, turned = both_columns(grad_spec)
    rows_ref[...] = jnp.zeros_like(rows_ref)
    put_halves(rows_ref, straight, turned)
    mixed_ref[...] = jnp.zeros_like(mixed_ref)
    for m in range(MODES):
        rows = rows_ref[m * 8 : (m + 1) * 8, :].astype(BF16)
        mixed_ref[m * 8 : (m + 1) * 8, :C] = dot_lanes(rows, weight_ref[m * C : (m + 1) * C, :])
    real = get_rows(mixed_ref, 0) + get_rows(mixed_ref, 2)
    imag = get_rows(mixed_ref, 1) + get_rows(mixed_ref, 3)
    modes = jnp.concatenate([real, imag], axis=0)
    out_ref[...] = first_inverse(modes * FORWARD_FACTOR, back_ref[...])


def weight_grad_body(
    mine_ref, other_ref, pairs_ref, out_ref, act_ref, left_ref, right_ref, wide
):
    left_ref[...] = jnp.zeros_like(left_ref)
    right_ref[...] = jnp.zeros_like(right_ref)
    for index, pack_ref in enumerate((mine_ref, other_ref)):
        straight, turned = both_columns(pack_ref[64:128, :])
        put_rows(left_ref, 2 * index, pack_ref[0:MODES, :])
        put_rows(left_ref, 2 * index + 1, pack_ref[MODES : 2 * MODES, :])
        put_rows(right_ref, 2 * index, straight)
        put_rows(right_ref, 2 * index + 1, turned)
    for m in range(MODES):
        rows = slice(m * 8, (m + 1) * 8)
        out_ref[m * C : (m + 1) * C, :] = dot_rows(
            left_ref[rows, :], right_ref[rows, :], lax.Precision.HIGHEST
        )[:C]
    for pair in range(2):
        for y in range(8):
            put_cell_pair(wide, y, pairs_ref[block(y, pair)].astype(F32))
        act_ref[:, pair * 16 : (pair + 1) * 16, :] = (
            wide[...].astype(BF16).reshape(C, 16, 128)
        )


ERFC = (
    0.17087277,
    -0.82215223,
    1.48851587,
    -1.13520398,
    0.27886807,
    -0.18628806,
    0.09678418,
    0.37409196,
    1.00002368,
    -1.26551223,
)


def gelu_and_slope(pre):
    bell = jnp.exp(-0.5 * pre * pre)
    t = 1.0 / (1.0 + (0.5 / math.sqrt(2.0)) * jnp.abs(pre))
    series = jnp.full_like(t, ERFC[0])
    for coefficient in ERFC[1:]:
        series = series * t + coefficient
    tail = (0.5 * t) * (jnp.exp(series) * bell)
    cumulative = jnp.where(pre < 0.0, tail, 1.0 - tail)
    return pre * cumulative, cumulative + pre * (bell * (1.0 / math.sqrt(2.0 * math.pi)))


def middle_body(
    in_ref, pairs_ref, cotangent_ref, weight_ref, column_ref, table_ref, act_ref, grad_ref,
    out_ref, wide,
):
    weight = weight_ref[...]
    bias = jnp.concatenate([column_ref[...]] * MIDDLE_GROUP, axis=0)
    back = table_ref[DEPTH_BACK]
    table = table_ref[DEPTH]
    for pair in range(2):
        part = cotangent_ref[:, pair * 16 : (pair + 1) * 16, :]
        wide[...] = part.astype(F32).reshape(C * 16, 128)
        for ys in y_groups(MIDDLE_GROUP):
            pre = back_and_local(in_ref, back, weight, pairs_ref, ys, pair) + bias
            activation, slope = gelu_and_slope(pre)
            cotangent = jnp.concatenate([cell_pair(wide, y) for y in ys], axis=0)
            activation = activation.astype(BF16)
            grad_pre = (cotangent * slope).astype(BF16)
            send_depth(table, grad_pre, out_ref, ys, pair)
            for i, y in enumerate(ys):
                act_ref[block(y, pair)] = activation[i * 128 : (i + 1) * 128]
                grad_ref[block(y, pair)] = grad_pre[i * 128 : (i + 1) * 128]


def last_body(in_ref, grad_ref, weight_ref, table_ref, out_ref, wide, cells_ref, sems):
    back = table_ref[DEPTH_BACK]
    weight = both_cells(weight_ref[...].astype(F32))
    copies = []
    for pair in range(2):
        for ys in y_groups(LAST_GROUP):
            total = back_and_local(in_ref, back, weight, grad_ref, ys, pair)
            for i, y in enumerate(ys):
                put_cell_pair(wide, y, total[i * 128 : (i + 1) * 128])
        cells_ref[pair] = wide[...].astype(BF16).reshape(C, 16, 128)
        copies.append(
            pltpu.make_async_copy(cells_ref.at[pair], part_of(out_ref, pair), sems.at[pair])
        )
        copies[pair].start()
    for copy in copies:
        copy.wait()


def over_py(values):
    return lax.all_to_all(
        values.reshape(PY, 64, 128), "py", 0, 0, tiled=True, axis_index_groups=[list(PY_ORDER)]
    )


def over_px(values):
    return lax.all_to_all(values.reshape(PX, 8, 128), "px", 0, 0, tiled=True).reshape(128, 128)


def shards(fields, cotangent, spectral_weight, local_weight, bias_term):
    small = small_tables()
    first_table, first_back = first_tables()
    weight = spectral_weight.reshape(MODES * C, 128)
    wide = pltpu.VMEM((C * 16, 128), F32)
    halves_of_cells = pltpu.VMEM((2, C, 16, 128), BF16)
    rows = pltpu.VMEM((MODES * 8, 128), F32)
    cells = C * CELLS
    grid = jax.ShapeDtypeStruct((C, CELLS, 128), BF16)
    in_place = pl.BlockSpec(memory_space=pltpu.HBM)
    second_forward = call(second_forward_body, shape(128), "y_forward")
    second_inverse = call(
        second_inverse_body, jax.ShapeDtypeStruct((PY, 64, 128), F32), "y_inverse"
    )

    pairs, sent = call(
        depth_body,
        (shape(256, BF16, 1024), shape(512)),
        "z_forward",
        [wide],
    )(fields.reshape(C, CELLS, 128))
    received = over_px(second_forward(over_py(sent), small))
    sent, spectrum, turned, column = call(
        mix_body,
        (shape(128), shape(64), shape(128, BF16), shape(128)),
        "modes_mix",
        [rows, rows],
    )(received, weight, first_table, first_back, local_weight, bias_term.reshape(1, C))
    received = over_py(second_inverse(over_px(sent), small))
    activation, grad_pre, sent = call(
        middle_body,
        (shape(256, BF16, 1024), shape(256, BF16, 1024), shape(512)),
        "gelu_z",
        [wide],
    )(
        received.reshape(512, 128),
        pairs,
        cotangent.reshape(C, CELLS, 128),
        turned,
        column,
        small,
    )
    received = over_px(second_forward(over_py(sent), small))
    sent, pack = call(mix_back_body, (shape(128), shape(128)), "modes_back", [rows, rows])(
        received, weight, spectrum, first_table, first_back
    )
    received = over_px(sent)
    other = lax.ppermute(pack, "pair", [(0, 1), (1, 0)])
    weight_grad, activation = call(
        weight_grad_body,
        (shape(MODES * C), grid),
        "weight_grad",
        [rows, rows, wide],
        flops=10**8,
        nbytes=10**6,
    )(pack, other, activation)
    received = over_py(second_inverse(received, small))
    input_grad = call(
        last_body,
        grid,
        "z_inverse",
        [wide, halves_of_cells, pltpu.SemaphoreType.DMA((2,))],
        out_specs=in_place,
    )(received.reshape(512, 128), grad_pre, local_weight, small)
    return (
        activation.reshape(fields.shape),
        input_grad.reshape(fields.shape),
        weight_grad.reshape(spectral_weight.shape),
    )


def solution(mesh):
    grid = P("pair", None, "px", "py", None)
    modes = P("px", "py", None, None, None)
    return jax.shard_map(
        shards,
        mesh=mesh,
        in_specs=(grid, grid, modes, P(), P()),
        out_specs=(grid, grid, modes),
        check_vma=False,
    )
```

```python
import math

import jax
import jax.numpy as jnp
import ml_dtypes
import numpy as np
from jax import lax
from jax.experimental import pallas as pl
from jax.experimental.pallas import tpu as pltpu
from jax.sharding import PartitionSpec as P

C = 64
KX = 16
KY = 16
KZ = 16
NX = 64
NY = 64
NZ = 128
PX = 16
PY = 8
CELLS = 32
MODES = 32
FORWARD_FACTOR = 1.0 / math.sqrt(NX * NY * NZ)
INVERSE_FACTOR = 1.0 / math.sqrt(KX * KY * KZ)
F32 = jnp.float32
BF16 = jnp.bfloat16
PY_ORDER = (6, 2, 5, 1, 7, 3, 4, 0)
MIDDLE_GROUP = 1
LAST_GROUP = 1


def cos_sin(cells, modes, length):
    phases = np.outer(np.arange(cells), np.arange(modes)) % length
    angles = phases * (2.0 * math.pi / length)
    return np.cos(angles), np.sin(angles)


def halves(table):
    table = table.astype(np.float32)
    high = table.astype(ml_dtypes.bfloat16)
    low = (table - high.astype(np.float32)).astype(ml_dtypes.bfloat16)
    return high, low


def stacked_table(table, axis):
    high, low = halves(table)
    return np.concatenate([high, high, low], axis=axis)


def depth_tables():
    cosine, sine = cos_sin(NZ, KZ, NZ)
    order = np.array([2 * peer + kz for kz in range(2) for peer in PY_ORDER])
    forward = np.concatenate([cosine.T[order], -sine.T[order]], axis=0)
    backward = np.concatenate([cosine.T[order], -sine.T[order]], axis=0)
    forward = forward.astype(np.float32).astype(ml_dtypes.bfloat16)
    return forward, stacked_table(backward, 0)


def second_tables():
    cosine, sine = cos_sin(NY, KY, NY)
    cells = np.array([8 * peer + cell for peer in PY_ORDER for cell in range(8)])
    cosine, sine = cosine[cells], sine[cells]
    forward = np.concatenate([cosine.T, sine.T], axis=0)
    backward = np.concatenate([cosine, sine], axis=1)
    return stacked_table(forward, 1), stacked_table(backward, 1)


def first_tables():
    cosine, sine = cos_sin(NX, KX, NX)
    by_x = [cosine.reshape(PX, 2, 2, KX), sine.reshape(PX, 2, 2, KX)]
    table = np.zeros((2, 2, 2, KX, PX, 2, 2, 2))
    for kz in range(2):
        turned = [np.transpose(t, (2, 3, 0, 1)) for t in by_x]
        table[:, 0, kz, :, :, 0, kz, :] = turned[0]
        table[:, 0, kz, :, :, 1, kz, :] = turned[1]
        table[:, 1, kz, :, :, 0, kz, :] = -turned[1]
        table[:, 1, kz, :, :, 1, kz, :] = turned[0]
    table = table.reshape(128, 128)
    return stacked_table(table, 1), stacked_table(table.T, 1)


def small_tables():
    pieces = depth_tables() + second_tables()
    rows = [np.pad(p, ((0, 0), (0, 256 - p.shape[1]))) for p in pieces]
    return np.concatenate(rows, axis=0)


DEPTH = (slice(0, 32), slice(0, 128))
DEPTH_BACK = (slice(32, 128), slice(0, 128))
SECOND = (slice(128, 160), slice(0, 192))
SECOND_BACK = (slice(160, 224), slice(0, 96))


def stacked(values):
    high = values.astype(BF16)
    low = (values - high.astype(F32)).astype(BF16)
    return jnp.concatenate([high, low, high], axis=0)


def dot(left, right):
    return jnp.dot(left, right, preferred_element_type=F32)


def dot_lanes(left, right):
    return lax.dot_general(left, right, (((1,), (1,)), ((), ())), preferred_element_type=F32)


def dot_rows(left, right, precision=None):
    return lax.dot_general(
        left, right, (((0,), (0,)), ((), ())), preferred_element_type=F32, precision=precision
    )


def call(body, outs, name, scratch=(), flops=0, nbytes=0, **specs):
    return pl.pallas_call(
        body,
        out_shape=outs,
        scratch_shapes=list(scratch),
        compiler_params=pltpu.CompilerParams(vmem_limit_bytes=24 * 1024 * 1024),
        cost_estimate=pl.CostEstimate(flops=flops, bytes_accessed=nbytes, transcendentals=0),
        name=name,
        **specs,
    )


def shape(rows, dtype=F32, lanes=128):
    return jax.ShapeDtypeStruct((rows, lanes), dtype)


def cell_pair(wide, y):
    parts = [wide[pl.ds(q * 8 + y, C, stride=16), :] for q in range(2)]
    return jnp.concatenate(parts, axis=0)


def put_cell_pair(wide, y, values):
    for q in range(2):
        wide[pl.ds(q * 8 + y, C, stride=16), :] = values[q * C : (q + 1) * C]


def block(y, pair):
    return slice(pair * 128, (pair + 1) * 128), slice(y * 128, (y + 1) * 128)


def send_depth(table, cells, out_ref, ys, pair):
    modes = dot_lanes(table, cells)
    for i, y in enumerate(ys):
        for g in range(4):
            out_ref[pl.ds((g * 2 + pair) * 8 + y, PY, stride=64), :] = modes[
                g * 8 : (g + 1) * 8, i * 128 : (i + 1) * 128
            ]


def depth_modes(ref, ys, pair):
    def one(y, g):
        return ref[pl.ds((g * 2 + pair) * 8 + y, PY, stride=64), :]

    return jnp.concatenate(
        [jnp.concatenate([one(y, g) for y in ys], axis=1) for g in range(4)], axis=0
    )


def back_and_local(in_ref, back, weight, cells_ref, ys, pair):
    total = dot_rows(stacked(depth_modes(in_ref, ys, pair)), back)
    rows = slice(pair * 128, (pair + 1) * 128)
    mixed = dot(weight, cells_ref[rows, ys[0] * 128 : (ys[-1] + 1) * 128])
    parts = [mixed[:, i * 128 : (i + 1) * 128] for i in range(len(ys))]
    return total + jnp.concatenate(parts, axis=0)


def both_cells(weight):
    zero = jnp.zeros_like(weight)
    return jnp.concatenate(
        [jnp.concatenate([weight, zero], axis=1), jnp.concatenate([zero, weight], axis=1)], axis=0
    ).astype(BF16)


def y_groups(size):
    return [list(range(first, first + size)) for first in range(0, 8, size)]


def part_of(ref, pair):
    return ref.at[:, pl.ds(pair * 16, 16), :]


def depth_table_here():
    row = lax.broadcasted_iota(jnp.int32, (32, 128), 0)
    cell = lax.broadcasted_iota(jnp.int32, (32, 128), 1)
    peer = sum(jnp.where(row % 8 == slot, peer, 0) for slot, peer in enumerate(PY_ORDER))
    wave = 2 * peer + (row // 8) % 2
    phase = (wave * cell + (NZ // 4) * (row // 16)) % NZ
    return jnp.cos(phase.astype(F32) * (2.0 * math.pi / NZ)).astype(BF16)


def depth_body(fields_ref, pairs_ref, out_ref, wide):
    table = depth_table_here()
    for pair in range(2):
        part = fields_ref[:, pair * 16 : (pair + 1) * 16, :]
        wide[...] = part.astype(F32).reshape(C * 16, 128)
        for y in range(8):
            cells = cell_pair(wide, y).astype(BF16)
            pairs_ref[block(y, pair)] = cells
            send_depth(table, cells, out_ref, [y], pair)


def second_forward_body(in_ref, table_ref, out_ref):
    table = table_ref[SECOND]
    turned = []
    for lb in range(8):
        column = in_ref[:, lb * 8 : (lb + 1) * 8, :].reshape(NY, 128)
        turned.append(dot(table, stacked(column)))
    for lb in range(4):
        real, imag = turned[lb], turned[lb + 4]
        out_ref[pl.ds(lb, KY, stride=8), :] = real[:KY] + imag[KY:]
        out_ref[pl.ds(lb + 4, KY, stride=8), :] = imag[:KY] - real[KY:]


def second_inverse_body(in_ref, table_ref, out_ref):
    table = table_ref[SECOND_BACK]
    columns = [in_ref[pl.ds(lb, KY, stride=8), :] for lb in range(8)]
    for lb in range(4):
        real, imag = columns[lb], columns[lb + 4]
        one = dot(table, stacked(jnp.concatenate([real, -imag], axis=0)))
        two = dot(table, stacked(jnp.concatenate([imag, real], axis=0)))
        out_ref[:, lb * 8 : (lb + 1) * 8, :] = one.reshape(PY, 8, 128)
        out_ref[:, (lb + 4) * 8 : (lb + 5) * 8, :] = two.reshape(PY, 8, 128)


def low_lanes(values):
    lane = lax.broadcasted_iota(jnp.int32, values.shape, 1)
    return jnp.where(lane < C, values, 0.0)


def swap_lanes(values):
    return pltpu.roll(values, C, 1)


def first_forward(values, table, factor):
    spread = dot(table, stacked(values))
    spectrum = spread[:64] + swap_lanes(spread[64:])
    return low_lanes(spectrum * factor)


def first_inverse(modes, table):
    low = low_lanes(modes)
    return dot(table, stacked(jnp.concatenate([low, swap_lanes(low)], axis=0)))


def put_rows(rows_ref, index, values):
    rows_ref[pl.ds(index, MODES, stride=8), :] = values


def get_rows(rows_ref, index):
    return rows_ref[pl.ds(index, MODES, stride=8), :]


def put_halves(rows_ref, real, imag):
    for index, values in enumerate((real, imag)):
        high = values.astype(BF16).astype(F32)
        put_rows(rows_ref, index, high)
        put_rows(rows_ref, index + 2, values - high)


def mix_body(
    in_ref, weight_ref, table_ref, back_ref, local_ref, bias_ref,
    out_ref, spectrum_ref, turned_ref, column_ref, rows_ref, mixed_ref,
):
    turned_ref[...] = both_cells(jnp.transpose(local_ref[...].astype(F32)))
    bias = jnp.transpose(jnp.broadcast_to(bias_ref[...], (128, C)))
    column_ref[...] = jnp.concatenate([bias, bias], axis=0)
    spectrum = first_forward(in_ref[...], table_ref[...], FORWARD_FACTOR)
    spectrum_ref[...] = spectrum
    rows_ref[...] = jnp.zeros_like(rows_ref)
    put_halves(rows_ref, spectrum[:MODES], spectrum[MODES:])
    for m in range(MODES):
        rows = rows_ref[m * 8 : (m + 1) * 8, :].astype(BF16)
        mixed_ref[m * 8 : (m + 1) * 8, :] = dot(rows[:, :C], weight_ref[m * C : (m + 1) * C, :])
    by_real = get_rows(mixed_ref, 0) + get_rows(mixed_ref, 2)
    by_imag = get_rows(mixed_ref, 1) + get_rows(mixed_ref, 3)
    mixed = jnp.concatenate(
        [by_real - swap_lanes(by_imag), swap_lanes(by_real) + by_imag], axis=0
    )
    out_ref[...] = first_inverse(mixed * INVERSE_FACTOR, back_ref[...])


def both_columns(spectrum):
    real, imag = spectrum[:MODES], spectrum[MODES:]
    return real + swap_lanes(imag), imag - swap_lanes(real)


def mix_back_body(
    in_ref, weight_ref, spectrum_ref, table_ref, back_ref, out_ref, pack_ref, rows_ref, mixed_ref
):
    grad_spec = first_forward(in_ref[...], table_ref[...], INVERSE_FACTOR)
    pack_ref[0:64, :] = spectrum_ref[...]
    pack_ref[64:128, :] = grad_spec
    straight, turned = both_columns(grad_spec)
    rows_ref[...] = jnp.zeros_like(rows_ref)
    put_halves(rows_ref, straight, turned)
    mixed_ref[...] = jnp.zeros_like(mixed_ref)
    for m in range(MODES):
        rows = rows_ref[m * 8 : (m + 1) * 8, :].astype(BF16)
        mixed_ref[m * 8 : (m + 1) * 8, :C] = dot_lanes(rows, weight_ref[m * C : (m + 1) * C, :])
    real = get_rows(mixed_ref, 0) + get_rows(mixed_ref, 2)
    imag = get_rows(mixed_ref, 1) + get_rows(mixed_ref, 3)
    modes = jnp.concatenate([real, imag], axis=0)
    out_ref[...] = first_inverse(modes * FORWARD_FACTOR, back_ref[...])


def weight_grad_body(
    mine_ref, other_ref, pairs_ref, out_ref, act_ref, left_ref, right_ref, wide
):
    left_ref[...] = jnp.zeros_like(left_ref)
    right_ref[...] = jnp.zeros_like(right_ref)
    for index, pack_ref in enumerate((mine_ref, other_ref)):
        straight, turned = both_columns(pack_ref[64:128, :])
        put_rows(left_ref, 2 * index, pack_ref[0:MODES, :])
        put_rows(left_ref, 2 * index + 1, pack_ref[MODES : 2 * MODES, :])
        put_rows(right_ref, 2 * index, straight)
        put_rows(right_ref, 2 * index + 1, turned)
    for m in range(MODES):
        rows = slice(m * 8, (m + 1) * 8)
        out_ref[m * C : (m + 1) * C, :] = dot_rows(
            left_ref[rows, :], right_ref[rows, :], lax.Precision.HIGHEST
        )[:C]
    for pair in range(2):
        for y in range(8):
            put_cell_pair(wide, y, pairs_ref[block(y, pair)].astype(F32))
        act_ref[:, pair * 16 : (pair + 1) * 16, :] = (
            wide[...].astype(BF16).reshape(C, 16, 128)
        )


ERFC = (
    0.17087277,
    -0.82215223,
    1.48851587,
    -1.13520398,
    0.27886807,
    -0.18628806,
    0.09678418,
    0.37409196,
    1.00002368,
    -1.26551223,
)


def gelu_and_slope(pre):
    bell = jnp.exp(-0.5 * pre * pre)
    t = 1.0 / (1.0 + (0.5 / math.sqrt(2.0)) * jnp.abs(pre))
    series = jnp.full_like(t, ERFC[0])
    for coefficient in ERFC[1:]:
        series = series * t + coefficient
    tail = (0.5 * t) * (jnp.exp(series) * bell)
    cumulative = jnp.where(pre < 0.0, tail, 1.0 - tail)
    return pre * cumulative, cumulative + pre * (bell * (1.0 / math.sqrt(2.0 * math.pi)))


def middle_body(
    in_ref, pairs_ref, cotangent_ref, weight_ref, column_ref, table_ref, act_ref, grad_ref,
    out_ref, wide,
):
    weight = weight_ref[...]
    bias = jnp.concatenate([column_ref[...]] * MIDDLE_GROUP, axis=0)
    back = table_ref[DEPTH_BACK]
    table = table_ref[DEPTH]
    for pair in range(2):
        part = cotangent_ref[:, pair * 16 : (pair + 1) * 16, :]
        wide[...] = part.astype(F32).reshape(C * 16, 128)
        for ys in y_groups(MIDDLE_GROUP):
            pre = back_and_local(in_ref, back, weight, pairs_ref, ys, pair) + bias
            activation, slope = gelu_and_slope(pre)
            cotangent = jnp.concatenate([cell_pair(wide, y) for y in ys], axis=0)
            activation = activation.astype(BF16)
            grad_pre = (cotangent * slope).astype(BF16)
            send_depth(table, grad_pre, out_ref, ys, pair)
            for i, y in enumerate(ys):
                act_ref[block(y, pair)] = activation[i * 128 : (i + 1) * 128]
                grad_ref[block(y, pair)] = grad_pre[i * 128 : (i + 1) * 128]


def last_body(in_ref, grad_ref, weight_ref, table_ref, out_ref, wide, cells_ref, sems):
    back = table_ref[DEPTH_BACK]
    weight = both_cells(weight_ref[...].astype(F32))
    copies = []
    for pair in range(2):
        for ys in y_groups(LAST_GROUP):
            total = back_and_local(in_ref, back, weight, grad_ref, ys, pair)
            for i, y in enumerate(ys):
                put_cell_pair(wide, y, total[i * 128 : (i + 1) * 128])
        cells_ref[pair] = wide[...].astype(BF16).reshape(C, 16, 128)
        copies.append(
            pltpu.make_async_copy(cells_ref.at[pair], part_of(out_ref, pair), sems.at[pair])
        )
        copies[pair].start()
    for copy in copies:
        copy.wait()


def over_py(values):
    return lax.all_to_all(
        values.reshape(PY, 64, 128), "py", 0, 0, tiled=True, axis_index_groups=[list(PY_ORDER)]
    )


def over_px(values):
    return lax.all_to_all(values.reshape(PX, 8, 128), "px", 0, 0, tiled=True).reshape(128, 128)


def shards(fields, cotangent, spectral_weight, local_weight, bias_term):
    small = small_tables()
    first_table, first_back = first_tables()
    weight = spectral_weight.reshape(MODES * C, 128)
    wide = pltpu.VMEM((C * 16, 128), F32)
    halves_of_cells = pltpu.VMEM((2, C, 16, 128), BF16)
    rows = pltpu.VMEM((MODES * 8, 128), F32)
    cells = C * CELLS
    grid = jax.ShapeDtypeStruct((C, CELLS, 128), BF16)
    in_place = pl.BlockSpec(memory_space=pltpu.HBM)
    second_forward = call(second_forward_body, shape(128), "y_forward")
    second_inverse = call(
        second_inverse_body, jax.ShapeDtypeStruct((PY, 64, 128), F32), "y_inverse"
    )

    pairs, sent = call(
        depth_body,
        (shape(256, BF16, 1024), shape(512)),
        "z_forward",
        [wide],
    )(fields.reshape(C, CELLS, 128))
    received = over_px(second_forward(over_py(sent), small))
    sent, spectrum, turned, column = call(
        mix_body,
        (shape(128), shape(64), shape(128, BF16), shape(128)),
        "modes_mix",
        [rows, rows],
    )(received, weight, first_table, first_back, local_weight, bias_term.reshape(1, C))
    received = over_py(second_inverse(over_px(sent), small))
    activation, grad_pre, sent = call(
        middle_body,
        (shape(256, BF16, 1024), shape(256, BF16, 1024), shape(512)),
        "gelu_z",
        [wide],
    )(
        received.reshape(512, 128),
        pairs,
        cotangent.reshape(C, CELLS, 128),
        turned,
        column,
        small,
    )
    received = over_px(second_forward(over_py(sent), small))
    sent, pack = call(mix_back_body, (shape(128), shape(128)), "modes_back", [rows, rows])(
        received, weight, spectrum, first_table, first_back
    )
    received = over_px(sent)
    other = lax.ppermute(pack, "pair", [(0, 1), (1, 0)])
    weight_grad, activation = call(
        weight_grad_body,
        (shape(MODES * C), grid),
        "weight_grad",
        [rows, rows, wide],
        flops=10**8,
        nbytes=10**6,
    )(pack, other, activation)
    received = over_py(second_inverse(received, small))
    input_grad = call(
        last_body,
        grid,
        "z_inverse",
        [wide, halves_of_cells, pltpu.SemaphoreType.DMA((2,))],
        out_specs=in_place,
    )(received.reshape(512, 128), grad_pre, local_weight, small)
    return (
        activation.reshape(fields.shape),
        input_grad.reshape(fields.shape),
        weight_grad.reshape(spectral_weight.shape),
    )


def solution(mesh):
    grid = P("pair", None, "px", "py", None)
    modes = P("px", "py", None, None, None)
    return jax.shard_map(
        shards,
        mesh=mesh,
        in_specs=(grid, grid, modes, P(), P()),
        out_specs=(grid, grid, modes),
        check_vma=False,
    )
```

```python
import math

import jax
import jax.numpy as jnp
import ml_dtypes
import numpy as np
from jax import lax
from jax.experimental import pallas as pl
from jax.experimental.pallas import tpu as pltpu
from jax.sharding import PartitionSpec as P

C = 64
KX = 16
KY = 16
KZ = 16
NX = 64
NY = 64
NZ = 128
PX = 16
PY = 8
CELLS = 32
MODES = 32
FORWARD_FACTOR = 1.0 / math.sqrt(NX * NY * NZ)
INVERSE_FACTOR = 1.0 / math.sqrt(KX * KY * KZ)
F32 = jnp.float32
BF16 = jnp.bfloat16
PY_ORDER = (7, 3, 6, 2, 0, 4, 5, 1)
MIDDLE_GROUP = 1
LAST_GROUP = 1


def cos_sin(cells, modes, length):
    phases = np.outer(np.arange(cells), np.arange(modes)) % length
    angles = phases * (2.0 * math.pi / length)
    return np.cos(angles), np.sin(angles)


def halves(table):
    table = table.astype(np.float32)
    high = table.astype(ml_dtypes.bfloat16)
    low = (table - high.astype(np.float32)).astype(ml_dtypes.bfloat16)
    return high, low


def stacked_table(table, axis):
    high, low = halves(table)
    return np.concatenate([high, high, low], axis=axis)


def depth_tables():
    cosine, sine = cos_sin(NZ, KZ, NZ)
    order = np.array([2 * peer + kz for kz in range(2) for peer in PY_ORDER])
    forward = np.concatenate([cosine.T[order], -sine.T[order]], axis=0)
    backward = np.concatenate([cosine.T[order], -sine.T[order]], axis=0)
    forward = forward.astype(np.float32).astype(ml_dtypes.bfloat16)
    return forward, stacked_table(backward, 0)


def second_tables():
    cosine, sine = cos_sin(NY, KY, NY)
    cells = np.array([8 * peer + cell for peer in PY_ORDER for cell in range(8)])
    cosine, sine = cosine[cells], sine[cells]
    forward = np.concatenate([cosine.T, sine.T], axis=0)
    backward = np.concatenate([cosine, sine], axis=1)
    return stacked_table(forward, 1), stacked_table(backward, 1)


def first_tables():
    cosine, sine = cos_sin(NX, KX, NX)
    by_x = [cosine.reshape(PX, 2, 2, KX), sine.reshape(PX, 2, 2, KX)]
    table = np.zeros((2, 2, 2, KX, PX, 2, 2, 2))
    for kz in range(2):
        turned = [np.transpose(t, (2, 3, 0, 1)) for t in by_x]
        table[:, 0, kz, :, :, 0, kz, :] = turned[0]
        table[:, 0, kz, :, :, 1, kz, :] = turned[1]
        table[:, 1, kz, :, :, 0, kz, :] = -turned[1]
        table[:, 1, kz, :, :, 1, kz, :] = turned[0]
    table = table.reshape(128, 128)
    return stacked_table(table, 1), stacked_table(table.T, 1)


def small_tables():
    pieces = depth_tables() + second_tables()
    rows = [np.pad(p, ((0, 0), (0, 256 - p.shape[1]))) for p in pieces]
    return np.concatenate(rows, axis=0)


DEPTH = (slice(0, 32), slice(0, 128))
DEPTH_BACK = (slice(32, 128), slice(0, 128))
SECOND = (slice(128, 160), slice(0, 192))
SECOND_BACK = (slice(160, 224), slice(0, 96))


def stacked(values):
    high = values.astype(BF16)
    low = (values - high.astype(F32)).astype(BF16)
    return jnp.concatenate([high, low, high], axis=0)


def dot(left, right):
    return jnp.dot(left, right, preferred_element_type=F32)


def dot_lanes(left, right):
    return lax.dot_general(left, right, (((1,), (1,)), ((), ())), preferred_element_type=F32)


def dot_rows(left, right, precision=None):
    return lax.dot_general(
        left, right, (((0,), (0,)), ((), ())), preferred_element_type=F32, precision=precision
    )


def call(body, outs, name, scratch=(), flops=0, nbytes=0, **specs):
    return pl.pallas_call(
        body,
        out_shape=outs,
        scratch_shapes=list(scratch),
        compiler_params=pltpu.CompilerParams(vmem_limit_bytes=24 * 1024 * 1024),
        cost_estimate=pl.CostEstimate(flops=flops, bytes_accessed=nbytes, transcendentals=0),
        name=name,
        **specs,
    )


def shape(rows, dtype=F32, lanes=128):
    return jax.ShapeDtypeStruct((rows, lanes), dtype)


def cell_pair(wide, y):
    parts = [wide[pl.ds(q * 8 + y, C, stride=16), :] for q in range(2)]
    return jnp.concatenate(parts, axis=0)


def put_cell_pair(wide, y, values):
    for q in range(2):
        wide[pl.ds(q * 8 + y, C, stride=16), :] = values[q * C : (q + 1) * C]


def block(y, pair):
    return slice(pair * 128, (pair + 1) * 128), slice(y * 128, (y + 1) * 128)


def send_depth(table, cells, out_ref, ys, pair):
    modes = dot_lanes(table, cells)
    for i, y in enumerate(ys):
        for g in range(4):
            out_ref[pl.ds((g * 2 + pair) * 8 + y, PY, stride=64), :] = modes[
                g * 8 : (g + 1) * 8, i * 128 : (i + 1) * 128
            ]


def depth_modes(ref, ys, pair):
    def one(y, g):
        return ref[pl.ds((g * 2 + pair) * 8 + y, PY, stride=64), :]

    return jnp.concatenate(
        [jnp.concatenate([one(y, g) for y in ys], axis=1) for g in range(4)], axis=0
    )


def back_and_local(in_ref, back, weight, cells_ref, ys, pair):
    total = dot_rows(stacked(depth_modes(in_ref, ys, pair)), back)
    rows = slice(pair * 128, (pair + 1) * 128)
    mixed = dot(weight, cells_ref[rows, ys[0] * 128 : (ys[-1] + 1) * 128])
    parts = [mixed[:, i * 128 : (i + 1) * 128] for i in range(len(ys))]
    return total + jnp.concatenate(parts, axis=0)


def both_cells(weight):
    zero = jnp.zeros_like(weight)
    return jnp.concatenate(
        [jnp.concatenate([weight, zero], axis=1), jnp.concatenate([zero, weight], axis=1)], axis=0
    ).astype(BF16)


def y_groups(size):
    return [list(range(first, first + size)) for first in range(0, 8, size)]


def part_of(ref, pair):
    return ref.at[:, pl.ds(pair * 16, 16), :]


def depth_table_here():
    row = lax.broadcasted_iota(jnp.int32, (32, 128), 0)
    cell = lax.broadcasted_iota(jnp.int32, (32, 128), 1)
    peer = sum(jnp.where(row % 8 == slot, peer, 0) for slot, peer in enumerate(PY_ORDER))
    wave = 2 * peer + (row // 8) % 2
    phase = (wave * cell + (NZ // 4) * (row // 16)) % NZ
    return jnp.cos(phase.astype(F32) * (2.0 * math.pi / NZ)).astype(BF16)


def depth_body(fields_ref, pairs_ref, out_ref, wide):
    table = depth_table_here()
    for pair in range(2):
        part = fields_ref[:, pair * 16 : (pair + 1) * 16, :]
        wide[...] = part.astype(F32).reshape(C * 16, 128)
        for y in range(8):
            cells = cell_pair(wide, y).astype(BF16)
            pairs_ref[block(y, pair)] = cells
            send_depth(table, cells, out_ref, [y], pair)


def second_forward_body(in_ref, table_ref, out_ref):
    table = table_ref[SECOND]
    turned = []
    for lb in range(8):
        column = in_ref[:, lb * 8 : (lb + 1) * 8, :].reshape(NY, 128)
        turned.append(dot(table, stacked(column)))
    for lb in range(4):
        real, imag = turned[lb], turned[lb + 4]
        out_ref[pl.ds(lb, KY, stride=8), :] = real[:KY] + imag[KY:]
        out_ref[pl.ds(lb + 4, KY, stride=8), :] = imag[:KY] - real[KY:]


def second_inverse_body(in_ref, table_ref, out_ref):
    table = table_ref[SECOND_BACK]
    columns = [in_ref[pl.ds(lb, KY, stride=8), :] for lb in range(8)]
    for lb in range(4):
        real, imag = columns[lb], columns[lb + 4]
        one = dot(table, stacked(jnp.concatenate([real, -imag], axis=0)))
        two = dot(table, stacked(jnp.concatenate([imag, real], axis=0)))
        out_ref[:, lb * 8 : (lb + 1) * 8, :] = one.reshape(PY, 8, 128)
        out_ref[:, (lb + 4) * 8 : (lb + 5) * 8, :] = two.reshape(PY, 8, 128)


def low_lanes(values):
    lane = lax.broadcasted_iota(jnp.int32, values.shape, 1)
    return jnp.where(lane < C, values, 0.0)


def swap_lanes(values):
    return pltpu.roll(values, C, 1)


def first_forward(values, table, factor):
    spread = dot(table, stacked(values))
    spectrum = spread[:64] + swap_lanes(spread[64:])
    return low_lanes(spectrum * factor)


def first_inverse(modes, table):
    low = low_lanes(modes)
    return dot(table, stacked(jnp.concatenate([low, swap_lanes(low)], axis=0)))


def put_rows(rows_ref, index, values):
    rows_ref[pl.ds(index, MODES, stride=8), :] = values


def get_rows(rows_ref, index):
    return rows_ref[pl.ds(index, MODES, stride=8), :]


def put_halves(rows_ref, real, imag):
    for index, values in enumerate((real, imag)):
        high = values.astype(BF16).astype(F32)
        put_rows(rows_ref, index, high)
        put_rows(rows_ref, index + 2, values - high)


def mix_body(
    in_ref, weight_ref, table_ref, back_ref, local_ref, bias_ref,
    out_ref, spectrum_ref, turned_ref, column_ref, rows_ref, mixed_ref,
):
    turned_ref[...] = both_cells(jnp.transpose(local_ref[...].astype(F32)))
    bias = jnp.transpose(jnp.broadcast_to(bias_ref[...], (128, C)))
    column_ref[...] = jnp.concatenate([bias, bias], axis=0)
    spectrum = first_forward(in_ref[...], table_ref[...], FORWARD_FACTOR)
    spectrum_ref[...] = spectrum
    rows_ref[...] = jnp.zeros_like(rows_ref)
    put_halves(rows_ref, spectrum[:MODES], spectrum[MODES:])
    for m in range(MODES):
        rows = rows_ref[m * 8 : (m + 1) * 8, :].astype(BF16)
        mixed_ref[m * 8 : (m + 1) * 8, :] = dot(rows[:, :C], weight_ref[m * C : (m + 1) * C, :])
    by_real = get_rows(mixed_ref, 0) + get_rows(mixed_ref, 2)
    by_imag = get_rows(mixed_ref, 1) + get_rows(mixed_ref, 3)
    mixed = jnp.concatenate(
        [by_real - swap_lanes(by_imag), swap_lanes(by_real) + by_imag], axis=0
    )
    out_ref[...] = first_inverse(mixed * INVERSE_FACTOR, back_ref[...])


def both_columns(spectrum):
    real, imag = spectrum[:MODES], spectrum[MODES:]
    return real + swap_lanes(imag), imag - swap_lanes(real)


def mix_back_body(
    in_ref, weight_ref, spectrum_ref, table_ref, back_ref, out_ref, pack_ref, rows_ref, mixed_ref
):
    grad_spec = first_forward(in_ref[...], table_ref[...], INVERSE_FACTOR)
    pack_ref[0:64, :] = spectrum_ref[...]
    pack_ref[64:128, :] = grad_spec
    straight, turned = both_columns(grad_spec)
    rows_ref[...] = jnp.zeros_like(rows_ref)
    put_halves(rows_ref, straight, turned)
    mixed_ref[...] = jnp.zeros_like(mixed_ref)
    for m in range(MODES):
        rows = rows_ref[m * 8 : (m + 1) * 8, :].astype(BF16)
        mixed_ref[m * 8 : (m + 1) * 8, :C] = dot_lanes(rows, weight_ref[m * C : (m + 1) * C, :])
    real = get_rows(mixed_ref, 0) + get_rows(mixed_ref, 2)
    imag = get_rows(mixed_ref, 1) + get_rows(mixed_ref, 3)
    modes = jnp.concatenate([real, imag], axis=0)
    out_ref[...] = first_inverse(modes * FORWARD_FACTOR, back_ref[...])


def weight_grad_body(
    mine_ref, other_ref, pairs_ref, out_ref, act_ref, left_ref, right_ref, wide
):
    left_ref[...] = jnp.zeros_like(left_ref)
    right_ref[...] = jnp.zeros_like(right_ref)
    for index, pack_ref in enumerate((mine_ref, other_ref)):
        straight, turned = both_columns(pack_ref[64:128, :])
        put_rows(left_ref, 2 * index, pack_ref[0:MODES, :])
        put_rows(left_ref, 2 * index + 1, pack_ref[MODES : 2 * MODES, :])
        put_rows(right_ref, 2 * index, straight)
        put_rows(right_ref, 2 * index + 1, turned)
    for m in range(MODES):
        rows = slice(m * 8, (m + 1) * 8)
        out_ref[m * C : (m + 1) * C, :] = dot_rows(
            left_ref[rows, :], right_ref[rows, :], lax.Precision.HIGHEST
        )[:C]
    for pair in range(2):
        for y in range(8):
            put_cell_pair(wide, y, pairs_ref[block(y, pair)].astype(F32))
        act_ref[:, pair * 16 : (pair + 1) * 16, :] = (
            wide[...].astype(BF16).reshape(C, 16, 128)
        )


ERFC = (
    0.17087277,
    -0.82215223,
    1.48851587,
    -1.13520398,
    0.27886807,
    -0.18628806,
    0.09678418,
    0.37409196,
    1.00002368,
    -1.26551223,
)


def gelu_and_slope(pre):
    bell = jnp.exp(-0.5 * pre * pre)
    t = 1.0 / (1.0 + (0.5 / math.sqrt(2.0)) * jnp.abs(pre))
    series = jnp.full_like(t, ERFC[0])
    for coefficient in ERFC[1:]:
        series = series * t + coefficient
    tail = (0.5 * t) * (jnp.exp(series) * bell)
    cumulative = jnp.where(pre < 0.0, tail, 1.0 - tail)
    return pre * cumulative, cumulative + pre * (bell * (1.0 / math.sqrt(2.0 * math.pi)))


def middle_body(
    in_ref, pairs_ref, cotangent_ref, weight_ref, column_ref, table_ref, act_ref, grad_ref,
    out_ref, wide,
):
    weight = weight_ref[...]
    bias = jnp.concatenate([column_ref[...]] * MIDDLE_GROUP, axis=0)
    back = table_ref[DEPTH_BACK]
    table = table_ref[DEPTH]
    for pair in range(2):
        part = cotangent_ref[:, pair * 16 : (pair + 1) * 16, :]
        wide[...] = part.astype(F32).reshape(C * 16, 128)
        for ys in y_groups(MIDDLE_GROUP):
            pre = back_and_local(in_ref, back, weight, pairs_ref, ys, pair) + bias
            activation, slope = gelu_and_slope(pre)
            cotangent = jnp.concatenate([cell_pair(wide, y) for y in ys], axis=0)
            activation = activation.astype(BF16)
            grad_pre = (cotangent * slope).astype(BF16)
            send_depth(table, grad_pre, out_ref, ys, pair)
            for i, y in enumerate(ys):
                act_ref[block(y, pair)] = activation[i * 128 : (i + 1) * 128]
                grad_ref[block(y, pair)] = grad_pre[i * 128 : (i + 1) * 128]


def last_body(in_ref, grad_ref, weight_ref, table_ref, out_ref, wide, cells_ref, sems):
    back = table_ref[DEPTH_BACK]
    weight = both_cells(weight_ref[...].astype(F32))
    copies = []
    for pair in range(2):
        for ys in y_groups(LAST_GROUP):
            total = back_and_local(in_ref, back, weight, grad_ref, ys, pair)
            for i, y in enumerate(ys):
                put_cell_pair(wide, y, total[i * 128 : (i + 1) * 128])
        cells_ref[pair] = wide[...].astype(BF16).reshape(C, 16, 128)
        copies.append(
            pltpu.make_async_copy(cells_ref.at[pair], part_of(out_ref, pair), sems.at[pair])
        )
        copies[pair].start()
    for copy in copies:
        copy.wait()


def over_py(values):
    return lax.all_to_all(
        values.reshape(PY, 64, 128), "py", 0, 0, tiled=True, axis_index_groups=[list(PY_ORDER)]
    )


def over_px(values):
    return lax.all_to_all(values.reshape(PX, 8, 128), "px", 0, 0, tiled=True).reshape(128, 128)


def shards(fields, cotangent, spectral_weight, local_weight, bias_term):
    small = small_tables()
    first_table, first_back = first_tables()
    weight = spectral_weight.reshape(MODES * C, 128)
    wide = pltpu.VMEM((C * 16, 128), F32)
    halves_of_cells = pltpu.VMEM((2, C, 16, 128), BF16)
    rows = pltpu.VMEM((MODES * 8, 128), F32)
    cells = C * CELLS
    grid = jax.ShapeDtypeStruct((C, CELLS, 128), BF16)
    in_place = pl.BlockSpec(memory_space=pltpu.HBM)
    second_forward = call(second_forward_body, shape(128), "y_forward")
    second_inverse = call(
        second_inverse_body, jax.ShapeDtypeStruct((PY, 64, 128), F32), "y_inverse"
    )

    pairs, sent = call(
        depth_body,
        (shape(256, BF16, 1024), shape(512)),
        "z_forward",
        [wide],
    )(fields.reshape(C, CELLS, 128))
    received = over_px(second_forward(over_py(sent), small))
    sent, spectrum, turned, column = call(
        mix_body,
        (shape(128), shape(64), shape(128, BF16), shape(128)),
        "modes_mix",
        [rows, rows],
    )(received, weight, first_table, first_back, local_weight, bias_term.reshape(1, C))
    received = over_py(second_inverse(over_px(sent), small))
    activation, grad_pre, sent = call(
        middle_body,
        (shape(256, BF16, 1024), shape(256, BF16, 1024), shape(512)),
        "gelu_z",
        [wide],
    )(
        received.reshape(512, 128),
        pairs,
        cotangent.reshape(C, CELLS, 128),
        turned,
        column,
        small,
    )
    received = over_px(second_forward(over_py(sent), small))
    sent, pack = call(mix_back_body, (shape(128), shape(128)), "modes_back", [rows, rows])(
        received, weight, spectrum, first_table, first_back
    )
    received = over_px(sent)
    other = lax.ppermute(pack, "pair", [(0, 1), (1, 0)])
    weight_grad, activation = call(
        weight_grad_body,
        (shape(MODES * C), grid),
        "weight_grad",
        [rows, rows, wide],
        flops=10**8,
        nbytes=10**6,
    )(pack, other, activation)
    received = over_py(second_inverse(received, small))
    input_grad = call(
        last_body,
        grid,
        "z_inverse",
        [wide, halves_of_cells, pltpu.SemaphoreType.DMA((2,))],
        out_specs=in_place,
    )(received.reshape(512, 128), grad_pre, local_weight, small)
    return (
        activation.reshape(fields.shape),
        input_grad.reshape(fields.shape),
        weight_grad.reshape(spectral_weight.shape),
    )


def solution(mesh):
    grid = P("pair", None, "px", "py", None)
    modes = P("px", "py", None, None, None)
    return jax.shard_map(
        shards,
        mesh=mesh,
        in_specs=(grid, grid, modes, P(), P()),
        out_specs=(grid, grid, modes),
        check_vma=False,
    )
```
